32 devices in a mesh: ep: 16 (over z, y, core), tp: 2 (over x).
Axes of the slice: x: 2, y: 2, z: 4, core: 2. Of those that a mesh axis runs over, the one named last changes fastest.
Arguments:
- tokens: bfloat16 [32, 256, 1280], P('ep', None, 'tp'), may hold values from -400 to 400
- router: bfloat16 [1280, 16], P('tp'), may hold values from -2 to 2
- w_in: bfloat16 [16, 1280, 2560], P('ep', None, 'tp'), may hold values from -0.15625 to 0.15625
- w_out: bfloat16 [16, 2560, 1280], P('ep', 'tp'), may hold values from -0.125 to 0.125
- grad_out: bfloat16 [32, 256, 1280], P('ep', None, 'tp'), may hold values from -6 to 6
Outputs:
- grad_tokens: bfloat16 [32, 256, 1280], P('ep', None, 'tp')
- grad_router: float32 [1280, 16], P('tp')
- grad_w_in: bfloat16 [16, 1280, 2560], P('ep', None, 'tp')
The draws below stay inside these ranges and needn't reach their ends.
All inputs are finite; a program needn't handle non-finite values.
Results may differ from the reference program's by a relative error of at most 0.0095.
Values may be sent and summed in bfloat16 or wider, within the bound.
A program may use at most 64 MiB of HBM per device.

```python
import math
from functools import partial
import jax
import jax.numpy as jnp
from jax import lax

D = 1280
FF = 2560
PATCHES = 256
IMAGES = 32
EXPERTS = 16


def router_columns(key, parity_weight):
    base = jax.random.fold_in(key, 11)
    values = jnp.clip(jax.random.normal(base, (D, EXPERTS), jnp.float32), -6.0, 6.0) * D ** (-0.5)
    rows = jnp.arange(D)[:, None] % 2
    cols = jnp.arange(EXPERTS)[None, :] % 2
    parity = (rows == cols).astype(jnp.float32) * math.sqrt(2.0)
    return values * (1.0 + parity_weight * parity)


def draw_router(key, part):
    columns = router_columns(key, 0.0)
    return jnp.clip(columns, -2.0, 2.0).astype(jnp.bfloat16)


def draw_tokens(key, part):
    key = jax.random.fold_in(key, 3)
    values = jnp.clip(jax.random.normal(key, (IMAGES, PATCHES, D), jnp.float32), -6.0, 6.0)
    return values.astype(jnp.bfloat16)


def level_of(key, shape, cuts, least, high):
    def one(axis_at, blocks):
        draws = jax.random.uniform(jax.random.fold_in(jax.random.fold_in(key, 6), axis_at), (blocks,), jnp.float32, least / len(cuts), high / len(cuts))
        return jnp.repeat(jnp.exp(draws), shape[axis_at] // blocks).reshape((-1,) + (1,) * (len(shape) - axis_at - 1))

    level = one(*cuts[0])
    for cut in cuts[1:]:
        level = level * one(*cut)
    return level


def noise(key, shape, deviation, reach, cuts=(), dtype=jnp.bfloat16):
    drawn = deviation * jax.random.normal(key, shape, jnp.float32)
    if cuts:
        drawn = drawn * level_of(key, shape, cuts, -0.22, 0.18)
    return jnp.clip(drawn, -reach, reach).astype(dtype)


def setup_inputs(seed: int = 0) -> dict:
    key_of = jax.random.split(jax.random.key(seed), 6)
    return {
        "tokens": draw_tokens(jax.random.fold_in(key_of[5], 71), 0),
        "router": draw_router(jax.random.fold_in(key_of[5], 71), 0),
        "w_in": noise(key_of[2], (EXPERTS, D, FF), D ** -0.5, 0.15625, ((0, 16), (2, 2))),
        "w_out": noise(key_of[3], (EXPERTS, FF, D), FF ** -0.5, 0.125, ((0, 16), (1, 2))),
        "grad_out": noise(key_of[4], (IMAGES, PATCHES, D), 1.0, 6.0, ((0, 16), (2, 2))),
    }


def expert_backward(items):
    slot_in, slot_grad, weight_in, weight_out = items
    pre = jnp.dot(slot_in, weight_in, preferred_element_type=jnp.float32)
    act, back = jax.vjp(partial(jax.nn.gelu, approximate=True), pre)
    slot_out = jnp.dot(act.astype(jnp.bfloat16), weight_out, preferred_element_type=jnp.float32).astype(jnp.bfloat16)
    act_grad = jnp.dot(slot_grad, weight_out.T, preferred_element_type=jnp.float32)
    pre_grad = back(act_grad)[0].astype(jnp.bfloat16)
    grad_weight = jnp.dot(slot_in.T, pre_grad, preferred_element_type=jnp.float32).astype(jnp.bfloat16)
    slot_in_grad = jnp.dot(pre_grad, weight_in.T, preferred_element_type=jnp.float32).astype(jnp.bfloat16)
    return (slot_out, grad_weight, slot_in_grad)

def reference(tokens, router, w_in, w_out, grad_out):
    tok32 = tokens.astype(jnp.float32)
    logits = jnp.einsum('bmd,de->bme', tok32, router.astype(jnp.float32))
    dispatch = jax.nn.softmax(logits, axis=1)
    combine = jax.nn.softmax(logits, axis=2)
    dispatch_b = dispatch.astype(jnp.bfloat16).astype(jnp.float32)
    combine_b = combine.astype(jnp.bfloat16).astype(jnp.float32)
    slot_in = jnp.einsum('bme,bmd->ebd', dispatch_b, tok32).astype(jnp.bfloat16)
    slot_grad = jnp.einsum('bme,bmd->ebd', combine_b, grad_out.astype(jnp.float32)).astype(jnp.bfloat16)
    slot_out, grad_w_in, slot_in_grad = lax.map(expert_backward, (slot_in, slot_grad, w_in, w_out))
    combine_dot = jnp.einsum('bmd,ebd->bme', grad_out.astype(jnp.float32), slot_out.astype(jnp.float32))
    grad_in32 = slot_in_grad.astype(jnp.float32)
    dispatch_dot = jnp.einsum('bmd,ebd->bme', tok32, grad_in32)
    logit_grad = combine * (combine_dot - lax.optimization_barrier(jnp.sum(combine * combine_dot, axis=2, keepdims=True)))
    logit_grad = logit_grad + dispatch * (dispatch_dot - lax.optimization_barrier(jnp.sum(dispatch * dispatch_dot, axis=1, keepdims=True)))
    logit_b = logit_grad.astype(jnp.bfloat16).astype(jnp.float32)
    grad_tokens = jnp.einsum('bme,ebd->bmd', dispatch_b, grad_in32)
    grad_tokens = grad_tokens + jnp.einsum('bme,de->bmd', logit_b, router.astype(jnp.float32))
    grad_router = jnp.einsum('bmd,bme->de', tok32, logit_b)
    return (grad_tokens.astype(jnp.bfloat16), grad_router, grad_w_in)
```

```python
import functools

import jax
import jax.numpy as jnp
from jax import lax
from jax.experimental import pallas as pl
from jax.experimental.pallas import tpu as pltpu
from jax.sharding import PartitionSpec as P

F32 = jnp.float32
BF16 = jnp.bfloat16
MESH = pl.DeviceIdType.MESH

LOGITS, SLOTS, OUT, IN, LOGIT_GRAD, SCATTER, GATHER = range(7)


def nt(a, b):
    return lax.dot_general(a, b, (((1,), (1,)), ((), ())), preferred_element_type=F32)


def tn(a, b):
    return lax.dot_general(a, b, (((0,), (0,)), ((), ())), preferred_element_type=F32)


def nn(a, b):
    return jnp.dot(a, b, preferred_element_type=F32)


def gelu_parts(v):
    c = 0.7978845608028654
    t = jnp.tanh(c * (v + 0.044715 * (v * v * v)))
    half = 0.5 * (1.0 + t)
    slope = half + (0.5 * c) * v * (1.0 - t * t) * (1.0 + (3.0 * 0.044715) * (v * v))
    return v * half, slope


def kernel(
    n_ep,
    tok_h, router_h, w_in_h, w_out_h, grad_h,
    grad_tokens_o, grad_router_o, grad_w_o,
    tok, router, w_in, w_out, grad,
    logits_s, logits_r, slots_s, slots_r, slot_in, slot_grad, pre_grad,
    out_s, out_r, in_s, in_r, lg_s, lg_r, rs_s, rs_r, ag,
    load_sem, send_sem, recv_sem,
):
    ep, tp = lax.axis_index("ep"), lax.axis_index("tp")
    other = 1 - tp
    n_all = 2 * n_ep
    me = tp * n_ep + ep
    images, patches, width = tok.shape
    experts = router.shape[0]
    rows = n_ep * images

    loads = [
        pltpu.make_async_copy(src, dst, load_sem.at[i])
        for i, (src, dst) in enumerate(
            ((tok_h, tok), (router_h, router), (grad_h, grad), (w_in_h, w_in), (w_out_h, w_out))
        )
    ]
    for load in loads:
        load.start()

    barrier = pltpu.get_barrier_semaphore()

    def greet(off, carry):
        q = lax.rem(me + off, n_all)
        pl.semaphore_signal(
            barrier, inc=1, device_id=(lax.rem(q, n_ep), q // n_ep), device_id_type=MESH
        )
        return carry

    lax.fori_loop(1, n_all, greet, 0)

    def to_partner(src, dst, k):
        return pltpu.make_async_remote_copy(
            src_ref=src, dst_ref=dst, send_sem=send_sem.at[k], recv_sem=recv_sem.at[k],
            device_id=(ep, other), device_id_type=MESH,
        )

    def send_all(src, by_expert, dst, k):
        def step(off, carry):
            q = lax.rem(me + off, n_all)
            to_ep, to_tp = lax.rem(q, n_ep), q // n_ep
            pltpu.make_async_remote_copy(
                src_ref=src.at[to_ep if by_expert else q], dst_ref=dst.at[me],
                send_sem=send_sem.at[k], recv_sem=recv_sem.at[k],
                device_id=(to_ep, to_tp), device_id_type=MESH,
            ).start()
            return carry

        lax.fori_loop(1, n_all, step, 0)

    def send_row(src, dst, k):
        def step(off, carry):
            to_ep = lax.rem(ep + off, n_ep)
            pltpu.make_async_remote_copy(
                src_ref=src(to_ep), dst_ref=dst.at[ep],
                send_sem=send_sem.at[k], recv_sem=recv_sem.at[k],
                device_id=(to_ep, tp), device_id_type=MESH,
            ).start()
            return carry

        lax.fori_loop(1, n_ep, step, 0)

    def wait_blocks(ref, count, sem):
        blocks = ref.at[pl.ds(0, count)]
        pltpu.make_async_copy(blocks, blocks, sem).wait()

    loads[0].wait()
    loads[1].wait()
    router_t = router[...]
    tok_rows = tok[...].reshape(images * patches, width)
    logits_s[...] = nt(router_t, tok_rows)
    pl.semaphore_wait(barrier, n_all - 1)
    swap = to_partner(logits_s, logits_r, LOGITS)
    swap.start()
    swap.wait()
    logits = logits_s[...] + logits_r[...]

    def per_image(x):
        return [x[:, b * patches : (b + 1) * patches] for b in range(images)]

    def softmax(x, axis):
        e = jnp.exp(x - jnp.max(x, axis=axis, keepdims=True))
        return e / jnp.sum(e, axis=axis, keepdims=True)

    dispatch = [softmax(x, 1) for x in per_image(logits)]
    combine = [softmax(x, 0) for x in per_image(logits)]
    dispatch_b = [x.astype(BF16) for x in dispatch]

    loads[2].wait()
    halves = [nn(dispatch_b[b], tok[b]) for b in range(images)]
    halves += [nn(combine[b].astype(BF16), grad[b]) for b in range(images)]
    slots_s[...] = jnp.stack(halves, axis=1).astype(BF16)
    slots_r[me] = slots_s[ep]
    send_all(slots_s, True, slots_r, SLOTS)

    loads[3].wait()
    loads[4].wait()
    wait_blocks(slots_r, n_all - 1, recv_sem.at[SLOTS])
    for s in range(2):
        half = slots_r[s * n_ep : (s + 1) * n_ep].astype(F32)
        cols = slice(s * width, (s + 1) * width)
        slot_in[:, cols] = half[:, :images].reshape(rows, width).astype(BF16)
        slot_grad[:, cols] = half[:, images:].reshape(rows, width).astype(BF16)

    def pieces(part, ref):
        for s in range(2):
            cut = part[:, s * width : (s + 1) * width]
            ref[s * n_ep : (s + 1) * n_ep] = cut.reshape(n_ep, images, width).astype(BF16)

    pre = nn(slot_in[...], w_in[...])
    act, slope = gelu_parts(pre)
    pieces(nn(act.astype(BF16), w_out[...]), out_s)
    out_r[me] = out_s[me]
    send_all(out_s, False, out_r, OUT)
    pre_grad[...] = (slope * nt(slot_grad[...], w_out[...])).astype(BF16)
    pieces(nt(pre_grad[...], w_in[...]), in_s)
    in_r[me] = in_s[me]
    send_all(in_s, False, in_r, IN)

    tile = 256 if grad_w_o.shape[0] % 256 == 0 else 128

    def grad_w_tile(i, carry):
        at = pl.ds(pl.multiple_of(i * tile, tile), tile)
        grad_w_o[at, :] = tn(slot_in[:, at], pre_grad[...]).astype(BF16)
        return carry

    lax.fori_loop(0, grad_w_o.shape[0] // tile, grad_w_tile, 0)

    def both_halves(ref):
        total = ref[:n_ep].astype(F32) + ref[n_ep:].astype(F32)
        return [total[:, b, :].astype(BF16) for b in range(images)]

    wait_blocks(out_r, n_all - 1, recv_sem.at[OUT])
    slot_out = both_halves(out_r)
    shares = []
    for b in range(images):
        dot = nt(slot_out[b], grad[b])
        shares.append(combine[b] * (dot - jnp.sum(combine[b] * dot, axis=0, keepdims=True)))
    wait_blocks(in_r, n_all - 1, recv_sem.at[IN])
    slot_in_grad = both_halves(in_r)
    for b in range(images):
        dot = nt(slot_in_grad[b], tok[b])
        shares[b] += dispatch[b] * (dot - jnp.sum(dispatch[b] * dot, axis=1, keepdims=True))
        lg_s[:, b * patches : (b + 1) * patches] = shares[b]
    swap_lg = to_partner(lg_s, lg_r, LOGIT_GRAD)
    swap_lg.start()
    swap_lg.wait()
    logit_b = (lg_s[...] + lg_r[...]).astype(BF16)

    part = nn(logit_b, tok_rows)
    rs_s[...] = part.reshape(n_ep, experts // n_ep, width)
    rs_r[ep] = rs_s[ep]
    send_row(lambda to_ep: rs_s.at[to_ep], rs_r, SCATTER)

    def tokens_of(b):
        left = jnp.concatenate([dispatch_b[b], per_image(logit_b)[b]], axis=0)
        right = jnp.concatenate([slot_in_grad[b], router_t], axis=0)
        grad_tokens_o[b] = tn(left, right).astype(BF16)

    for b in range(images // 2):
        tokens_of(b)
    wait_blocks(rs_r, n_ep - 1, recv_sem.at[SCATTER])
    ag[ep] = jnp.sum(rs_r[...], axis=0)
    send_row(lambda to_ep: ag.at[ep], ag, GATHER)
    for b in range(images // 2, images):
        tokens_of(b)
    wait_blocks(ag, n_ep - 1, recv_sem.at[GATHER])
    grad_router_o[...] = ag[...].reshape(experts, width)

    wait_blocks(slots_r, n_all - 1, send_sem.at[SLOTS])
    wait_blocks(out_r, n_all - 1, send_sem.at[OUT])
    wait_blocks(in_r, n_all - 1, send_sem.at[IN])
    wait_blocks(rs_r, n_ep - 1, send_sem.at[SCATTER])
    wait_blocks(ag, n_ep - 1, send_sem.at[GATHER])


def on_device(n_ep, tokens, router, w_in, w_out, grad_out):
    images, patches, width = tokens.shape
    experts = router.shape[1]
    w_in, w_out = w_in[0], w_out[0]
    model, hidden = w_in.shape
    rows = n_ep * images
    n_all = 2 * n_ep
    vmem = pltpu.VMEM
    grad_tokens, grad_router, grad_w = pl.pallas_call(
        functools.partial(kernel, n_ep),
        out_shape=(
            OUT_SPACE(tokens.shape, BF16),
            OUT_SPACE((experts, width), F32),
            OUT_SPACE(w_in.shape, BF16),
        ),
        in_specs=[pl.BlockSpec(memory_space=pltpu.HBM)] * 5,
        out_specs=(pl.BlockSpec(memory_space=pltpu.VMEM),) * 3,
        scratch_shapes=[
            vmem(tokens.shape, BF16),
            vmem((experts, width), BF16),
            vmem(w_in.shape, BF16),
            vmem(w_out.shape, BF16),
            vmem(grad_out.shape, BF16),
            vmem((experts, images * patches), F32),
            vmem((experts, images * patches), F32),
            vmem((experts, 2 * images, width), BF16),
            vmem((n_all, 2 * images, width), BF16),
            vmem((rows, model), BF16),
            vmem((rows, model), BF16),
            vmem((rows, hidden), BF16),
            vmem((n_all, images, width), BF16),
            vmem((n_all, images, width), BF16),
            vmem((n_all, images, width), BF16),
            vmem((n_all, images, width), BF16),
            vmem((experts, images * patches), F32),
            vmem((experts, images * patches), F32),
            vmem((n_ep, experts // n_ep, width), F32),
            vmem((n_ep, experts // n_ep, width), F32),
            vmem((n_ep, experts // n_ep, width), F32),
            pltpu.SemaphoreType.DMA((5,)),
            pltpu.SemaphoreType.DMA((7,)),
            pltpu.SemaphoreType.DMA((7,)),
        ],
        compiler_params=pltpu.CompilerParams(
            collective_id=0, has_side_effects=True, vmem_limit_bytes=40 * 1024 * 1024
        ),
    )(*(pltpu.with_memory_space_constraint(x, pltpu.HBM) for x in (tokens, router.T, w_in, w_out, grad_out)))
    return grad_tokens, grad_router.T, grad_w.reshape(1, model, hidden)


OUT_SPACE = pltpu.VMEM


def solution(mesh):
    placed = (
        P("ep", None, "tp"),
        P("tp", None),
        P("ep", None, "tp"),
        P("ep", "tp", None),
        P("ep", None, "tp"),
    )
    return jax.shard_map(
        functools.partial(on_device, mesh.shape["ep"]),
        mesh=mesh,
        in_specs=placed,
        out_specs=(P("ep", None, "tp"), P("tp", None), P("ep", None, "tp")),
        check_vma=False,
    )
```

```python
import functools

import jax
import jax.numpy as jnp
from jax import lax
from jax.experimental import pallas as pl
from jax.experimental.pallas import tpu as pltpu
from jax.sharding import PartitionSpec as P

F32 = jnp.float32
BF16 = jnp.bfloat16
MESH = pl.DeviceIdType.MESH

LOGITS, SLOTS, OUT, IN, LOGIT_GRAD, SCATTER, GATHER = range(7)


def nt(a, b):
    return lax.dot_general(a, b, (((1,), (1,)), ((), ())), preferred_element_type=F32)


def tn(a, b):
    return lax.dot_general(a, b, (((0,), (0,)), ((), ())), preferred_element_type=F32)


def nn(a, b):
    return jnp.dot(a, b, preferred_element_type=F32)


def gelu_parts(v):
    c = 0.7978845608028654
    t = jnp.tanh(c * (v + 0.044715 * (v * v * v)))
    half = 0.5 * (1.0 + t)
    slope = half + (0.5 * c) * v * (1.0 - t * t) * (1.0 + (3.0 * 0.044715) * (v * v))
    return v * half, slope


def kernel(
    n_ep,
    tok_h, router_h, w_in_h, w_out_h, grad_h,
    grad_tokens_o, grad_router_o, grad_w_o,
    tok, router, w_in, w_out, grad,
    logits_s, logits_r, slots_s, slots_r, slot_in, slot_grad, pre_grad,
    out_s, out_r, in_s, in_r, lg_s, lg_r, rs_s, rs_r, ag,
    load_sem, send_sem, recv_sem,
):
    ep, tp = lax.axis_index("ep"), lax.axis_index("tp")
    other = 1 - tp
    n_all = 2 * n_ep
    me = tp * n_ep + ep
    images, patches, width = tok.shape
    experts = router.shape[0]
    rows = n_ep * images

    loads = [
        pltpu.make_async_copy(src, dst, load_sem.at[i])
        for i, (src, dst) in enumerate(
            ((tok_h, tok), (router_h, router), (grad_h, grad), (w_in_h, w_in), (w_out_h, w_out))
        )
    ]
    for load in loads:
        load.start()

    barrier = pltpu.get_barrier_semaphore()

    def wrapped(off):
        to = ep + off
        return jnp.where(to >= n_ep, to - n_ep, to)

    def others(act):
        group = next(k for k in (5, 3, 1) if (n_ep - 1) % k == 0)

        def step(i, carry):
            for j in range(group):
                act(wrapped(i * group + (j + 1)))
            return carry

        lax.fori_loop(0, (n_ep - 1) // group, step, 0)

    def greet(to_ep, to_tp):
        pl.semaphore_signal(barrier, inc=1, device_id=(to_ep, to_tp), device_id_type=MESH)

    greet(ep, other)
    others(lambda to_ep: (greet(to_ep, tp), greet(to_ep, other)))

    def to_partner(src, dst, k):
        return pltpu.make_async_remote_copy(
            src_ref=src, dst_ref=dst, send_sem=send_sem.at[k], recv_sem=recv_sem.at[k],
            device_id=(ep, other), device_id_type=MESH,
        )

    def send_all(src, by_expert, dst, k):
        def send(to_ep, to_tp):
            pltpu.make_async_remote_copy(
                src_ref=src.at[to_ep if by_expert else to_tp * n_ep + to_ep], dst_ref=dst.at[me],
                send_sem=send_sem.at[k], recv_sem=recv_sem.at[k],
                device_id=(to_ep, to_tp), device_id_type=MESH,
            ).start()

        others(lambda to_ep: (send(to_ep, tp), send(to_ep, other)))
        send(ep, other)

    def send_row(src, dst, k):
        def send(to_ep):
            pltpu.make_async_remote_copy(
                src_ref=src(to_ep), dst_ref=dst.at[ep],
                send_sem=send_sem.at[k], recv_sem=recv_sem.at[k],
                device_id=(to_ep, tp), device_id_type=MESH,
            ).start()

        others(send)

    def wait_blocks(ref, count, sem):
        blocks = ref.at[pl.ds(0, count)]
        pltpu.make_async_copy(blocks, blocks, sem).wait()

    loads[0].wait()
    loads[1].wait()
    router_t = router[...]
    tok_rows = tok[...].reshape(images * patches, width)
    logits_s[...] = nt(router_t, tok_rows)
    pl.semaphore_wait(barrier, n_all - 1)
    swap = to_partner(logits_s, logits_r, LOGITS)
    swap.start()
    swap.wait()
    logits = logits_s[...] + logits_r[...]

    def per_image(x):
        return [x[:, b * patches : (b + 1) * patches] for b in range(images)]

    def softmax(x, axis):
        e = jnp.exp(x - jnp.max(x, axis=axis, keepdims=True))
        return e / jnp.sum(e, axis=axis, keepdims=True)

    dispatch = [softmax(x, 1) for x in per_image(logits)]
    combine = [softmax(x, 0) for x in per_image(logits)]
    dispatch_b = [x.astype(BF16) for x in dispatch]

    loads[2].wait()
    halves = [nn(dispatch_b[b], tok[b]) for b in range(images)]
    halves += [nn(combine[b].astype(BF16), grad[b]) for b in range(images)]
    slots_s[...] = jnp.stack(halves, axis=1).astype(BF16)
    slots_r[me] = slots_s[ep]
    send_all(slots_s, True, slots_r, SLOTS)

    loads[3].wait()
    loads[4].wait()
    wait_blocks(slots_r, n_all - 1, recv_sem.at[SLOTS])
    for s in range(2):
        half = slots_r[s * n_ep : (s + 1) * n_ep].astype(F32)
        cols = slice(s * width, (s + 1) * width)
        slot_in[:, cols] = half[:, :images].reshape(rows, width).astype(BF16)
        slot_grad[:, cols] = half[:, images:].reshape(rows, width).astype(BF16)

    def pieces(part, ref):
        for s in range(2):
            cut = part[:, s * width : (s + 1) * width]
            ref[s * n_ep : (s + 1) * n_ep] = cut.reshape(n_ep, images, width).astype(BF16)

    pre = nn(slot_in[...], w_in[...])
    act, slope = gelu_parts(pre)
    pieces(nn(act.astype(BF16), w_out[...]), out_s)
    out_r[me] = out_s[me]
    send_all(out_s, False, out_r, OUT)
    pre_grad[...] = (slope * nt(slot_grad[...], w_out[...])).astype(BF16)
    pieces(nt(pre_grad[...], w_in[...]), in_s)
    in_r[me] = in_s[me]
    send_all(in_s, False, in_r, IN)

    tile = 256 if grad_w_o.shape[0] % 256 == 0 else 128

    def grad_w_tile(i, carry):
        at = pl.ds(pl.multiple_of(i * tile, tile), tile)
        grad_w_o[at, :] = tn(slot_in[:, at], pre_grad[...]).astype(BF16)
        return carry

    lax.fori_loop(0, grad_w_o.shape[0] // tile, grad_w_tile, 0)

    def both_halves(ref):
        total = ref[:n_ep].astype(F32) + ref[n_ep:].astype(F32)
        return [total[:, b, :].astype(BF16) for b in range(images)]

    wait_blocks(out_r, n_all - 1, recv_sem.at[OUT])
    slot_out = both_halves(out_r)
    shares = []
    for b in range(images):
        dot = nt(slot_out[b], grad[b])
        shares.append(combine[b] * (dot - jnp.sum(combine[b] * dot, axis=0, keepdims=True)))
    wait_blocks(in_r, n_all - 1, recv_sem.at[IN])
    slot_in_grad = both_halves(in_r)
    for b in range(images):
        dot = nt(slot_in_grad[b], tok[b])
        shares[b] += dispatch[b] * (dot - jnp.sum(dispatch[b] * dot, axis=1, keepdims=True))
        lg_s[:, b * patches : (b + 1) * patches] = shares[b]
    swap_lg = to_partner(lg_s, lg_r, LOGIT_GRAD)
    swap_lg.start()
    swap_lg.wait()
    logit_b = (lg_s[...] + lg_r[...]).astype(BF16)

    part = nn(logit_b, tok_rows)
    rs_s[...] = part.reshape(n_ep, experts // n_ep, width)
    rs_r[ep] = rs_s[ep]
    send_row(lambda to_ep: rs_s.at[to_ep], rs_r, SCATTER)

    def tokens_of(b):
        left = jnp.concatenate([dispatch_b[b], per_image(logit_b)[b]], axis=0)
        right = jnp.concatenate([slot_in_grad[b], router_t], axis=0)
        grad_tokens_o[b] = tn(left, right).astype(BF16)

    for b in range(images // 2):
        tokens_of(b)
    wait_blocks(rs_r, n_ep - 1, recv_sem.at[SCATTER])
    ag[ep] = jnp.sum(rs_r[...], axis=0)
    send_row(lambda to_ep: ag.at[ep], ag, GATHER)
    for b in range(images // 2, images):
        tokens_of(b)
    wait_blocks(ag, n_ep - 1, recv_sem.at[GATHER])
    grad_router_o[...] = ag[...].reshape(experts, width)

    wait_blocks(slots_r, n_all - 1, send_sem.at[SLOTS])
    wait_blocks(out_r, n_all - 1, send_sem.at[OUT])
    wait_blocks(in_r, n_all - 1, send_sem.at[IN])
    wait_blocks(rs_r, n_ep - 1, send_sem.at[SCATTER])
    wait_blocks(ag, n_ep - 1, send_sem.at[GATHER])


def write_out(tokens_v, router_v, w_v, tokens_o, router_o, w_o, sem):
    cut = w_v.shape[0] // 4
    pairs = [(w_v.at[pl.ds(i * cut, cut)], w_o.at[pl.ds(i * cut, cut)]) for i in range(4)]
    pairs += [(tokens_v, tokens_o), (router_v, router_o)]
    copies = [pltpu.make_async_copy(a, b, sem.at[i]) for i, (a, b) in enumerate(pairs)]
    for copy in copies:
        copy.start()
    for copy in copies:
        copy.wait()


def on_device(n_ep, tokens, router, w_in, w_out, grad_out):
    images, patches, width = tokens.shape
    experts = router.shape[1]
    w_in, w_out = w_in[0], w_out[0]
    model, hidden = w_in.shape
    rows = n_ep * images
    n_all = 2 * n_ep
    vmem = pltpu.VMEM
    grad_tokens, grad_router, grad_w = pl.pallas_call(
        functools.partial(kernel, n_ep),
        out_shape=(
            pltpu.VMEM(tokens.shape, BF16),
            pltpu.VMEM((experts, width), F32),
            pltpu.VMEM(w_in.shape, BF16),
        ),
        in_specs=[pl.BlockSpec(memory_space=pltpu.HBM)] * 5,
        out_specs=(pl.BlockSpec(memory_space=pltpu.VMEM),) * 3,
        scratch_shapes=[
            vmem(tokens.shape, BF16),
            vmem((experts, width), BF16),
            vmem(w_in.shape, BF16),
            vmem(w_out.shape, BF16),
            vmem(grad_out.shape, BF16),
            vmem((experts, images * patches), F32),
            vmem((experts, images * patches), F32),
            vmem((experts, 2 * images, width), BF16),
            vmem((n_all, 2 * images, width), BF16),
            vmem((rows, model), BF16),
            vmem((rows, model), BF16),
            vmem((rows, hidden), BF16),
            vmem((n_all, images, width), BF16),
            vmem((n_all, images, width), BF16),
            vmem((n_all, images, width), BF16),
            vmem((n_all, images, width), BF16),
            vmem((experts, images * patches), F32),
            vmem((experts, images * patches), F32),
            vmem((n_ep, experts // n_ep, width), F32),
            vmem((n_ep, experts // n_ep, width), F32),
            vmem((n_ep, experts // n_ep, width), F32),
            pltpu.SemaphoreType.DMA((5,)),
            pltpu.SemaphoreType.DMA((7,)),
            pltpu.SemaphoreType.DMA((7,)),
        ],
        compiler_params=pltpu.CompilerParams(
            collective_id=0, has_side_effects=True, vmem_limit_bytes=40 * 1024 * 1024
        ),
    )(*(pltpu.with_memory_space_constraint(x, pltpu.HBM) for x in (tokens, router.T, w_in, w_out, grad_out)))
    results = (grad_tokens, grad_router, grad_w)
    grad_tokens, grad_router, grad_w = pl.pallas_call(
        write_out,
        out_shape=tuple(jax.ShapeDtypeStruct(x.shape, x.dtype) for x in results),
        in_specs=[pl.BlockSpec(memory_space=pltpu.VMEM)] * 3,
        out_specs=(pl.BlockSpec(memory_space=pltpu.HBM),) * 3,
        scratch_shapes=[pltpu.SemaphoreType.DMA((6,))],
    )(*results)
    return grad_tokens, grad_router.T, grad_w.reshape(1, model, hidden)


def solution(mesh):
    placed = (
        P("ep", None, "tp"),
        P("tp", None),
        P("ep", None, "tp"),
        P("ep", "tp", None),
        P("ep", None, "tp"),
    )
    return jax.shard_map(
        functools.partial(on_device, mesh.shape["ep"]),
        mesh=mesh,
        in_specs=placed,
        out_specs=(P("ep", None, "tp"), P("tp", None), P("ep", None, "tp")),
        check_vma=False,
    )
```

```python
import functools

import jax
import jax.numpy as jnp
from jax import lax
from jax.experimental import pallas as pl
from jax.experimental.pallas import tpu as pltpu
from jax.sharding import PartitionSpec as P

F32 = jnp.float32
BF16 = jnp.bfloat16
MESH = pl.DeviceIdType.MESH

LOGITS, SLOTS, GRADS, OUT, IN, LOGIT_GRAD, SCATTER, GATHER = range(8)


def nt(a, b):
    return lax.dot_general(a, b, (((1,), (1,)), ((), ())), preferred_element_type=F32)


def tn(a, b):
    return lax.dot_general(a, b, (((0,), (0,)), ((), ())), preferred_element_type=F32)


def nn(a, b):
    return jnp.dot(a, b, preferred_element_type=F32)


def gelu_parts(v):
    c = 0.7978845608028654
    t = jnp.tanh(c * (v + 0.044715 * (v * v * v)))
    half = 0.5 * (1.0 + t)
    slope = half + (0.5 * c) * v * (1.0 - t * t) * (1.0 + (3.0 * 0.044715) * (v * v))
    return v * half, slope


def kernel(
    n_ep,
    tok_h, router_h, w_in_h, w_out_h, grad_h,
    grad_tokens_o, grad_router_o, grad_w_o,
    tok, router, w_in, w_out, grad,
    logits_s, logits_r, slots_s, slots_r, grads_s, grads_r, slot_in, slot_grad, pre_grad,
    out_s, out_r, in_s, in_r, lg_s, lg_r, rs_s, rs_r, ag,
    load_sem, send_sem, recv_sem,
):
    ep, tp = lax.axis_index("ep"), lax.axis_index("tp")
    other = 1 - tp
    n_all = 2 * n_ep
    me = tp * n_ep + ep
    images, patches, width = tok.shape
    experts = router.shape[0]
    rows = n_ep * images

    loads = [
        pltpu.make_async_copy(src, dst, load_sem.at[i])
        for i, (src, dst) in enumerate(
            ((tok_h, tok), (router_h, router), (grad_h, grad), (w_in_h, w_in), (w_out_h, w_out))
        )
    ]
    for load in loads:
        load.start()

    barrier = pltpu.get_barrier_semaphore()

    def wrapped(off):
        to = ep + off
        return jnp.where(to >= n_ep, to - n_ep, to)

    def others(act):
        group = next(k for k in (5, 3, 1) if (n_ep - 1) % k == 0)

        def step(i, carry):
            for j in range(group):
                act(wrapped(i * group + (j + 1)))
            return carry

        lax.fori_loop(0, (n_ep - 1) // group, step, 0)

    def greet(to_ep, to_tp):
        pl.semaphore_signal(barrier, inc=1, device_id=(to_ep, to_tp), device_id_type=MESH)

    greet(ep, other)
    others(lambda to_ep: (greet(to_ep, tp), greet(to_ep, other)))

    def to_partner(src, dst, k):
        return pltpu.make_async_remote_copy(
            src_ref=src, dst_ref=dst, send_sem=send_sem.at[k], recv_sem=recv_sem.at[k],
            device_id=(ep, other), device_id_type=MESH,
        )

    def send_all(src, by_expert, dst, k):
        def send(to_ep, to_tp):
            pltpu.make_async_remote_copy(
                src_ref=src.at[to_ep if by_expert else to_tp * n_ep + to_ep], dst_ref=dst.at[me],
                send_sem=send_sem.at[k], recv_sem=recv_sem.at[k],
                device_id=(to_ep, to_tp), device_id_type=MESH,
            ).start()

        others(lambda to_ep: (send(to_ep, tp), send(to_ep, other)))
        send(ep, other)

    def send_row(src, dst, k):
        def send(to_ep):
            pltpu.make_async_remote_copy(
                src_ref=src(to_ep), dst_ref=dst.at[ep],
                send_sem=send_sem.at[k], recv_sem=recv_sem.at[k],
                device_id=(to_ep, tp), device_id_type=MESH,
            ).start()

        others(send)

    def wait_blocks(ref, count, sem):
        blocks = ref.at[pl.ds(0, count)]
        pltpu.make_async_copy(blocks, blocks, sem).wait()

    loads[0].wait()
    loads[1].wait()
    router_t = router[...]
    tok_rows = tok[...].reshape(images * patches, width)
    logits_s[...] = nt(router_t, tok_rows)
    pl.semaphore_wait(barrier, n_all - 1)
    swap = to_partner(logits_s, logits_r, LOGITS)
    swap.start()
    swap.wait()
    logits = logits_s[...] + logits_r[...]

    def per_image(x):
        return [x[:, b * patches : (b + 1) * patches] for b in range(images)]

    def softmax(x, axis):
        e = jnp.exp(x - jnp.max(x, axis=axis, keepdims=True))
        return e / jnp.sum(e, axis=axis, keepdims=True)

    dispatch = [softmax(x, 1) for x in per_image(logits)]
    combine = [softmax(x, 0) for x in per_image(logits)]
    dispatch_b = [x.astype(BF16) for x in dispatch]

    def halves(weights, rows_of, ref_s, ref_r, k):
        parts = [nn(weights[b], rows_of[b]) for b in range(images)]
        ref_s[...] = jnp.stack(parts, axis=1).astype(BF16)
        ref_r[me] = ref_s[ep]
        send_all(ref_s, True, ref_r, k)

    halves(dispatch_b, tok, slots_s, slots_r, SLOTS)
    loads[2].wait()
    halves([x.astype(BF16) for x in combine], grad, grads_s, grads_r, GRADS)

    def arrived(ref, dst, k):
        wait_blocks(ref, n_all - 1, recv_sem.at[k])
        for s in range(2):
            half = ref[s * n_ep : (s + 1) * n_ep].astype(F32)
            dst[:, s * width : (s + 1) * width] = half.reshape(rows, width).astype(BF16)

    loads[3].wait()
    loads[4].wait()
    arrived(slots_r, slot_in, SLOTS)

    def pieces(part, ref):
        for s in range(2):
            cut = part[:, s * width : (s + 1) * width]
            ref[s * n_ep : (s + 1) * n_ep] = cut.reshape(n_ep, images, width).astype(BF16)

    pre = nn(slot_in[...], w_in[...])
    act, slope = gelu_parts(pre)
    pieces(nn(act.astype(BF16), w_out[...]), out_s)
    out_r[me] = out_s[me]
    send_all(out_s, False, out_r, OUT)
    arrived(grads_r, slot_grad, GRADS)
    pre_grad[...] = (slope * nt(slot_grad[...], w_out[...])).astype(BF16)
    pieces(nt(pre_grad[...], w_in[...]), in_s)
    in_r[me] = in_s[me]
    send_all(in_s, False, in_r, IN)

    tile = 256 if grad_w_o.shape[0] % 256 == 0 else 128

    def grad_w_tile(i, carry):
        at = pl.ds(pl.multiple_of(i * tile, tile), tile)
        grad_w_o[at, :] = tn(slot_in[:, at], pre_grad[...]).astype(BF16)
        return carry

    lax.fori_loop(0, grad_w_o.shape[0] // tile, grad_w_tile, 0)

    def both_halves(ref):
        total = ref[:n_ep].astype(F32) + ref[n_ep:].astype(F32)
        return [total[:, b, :].astype(BF16) for b in range(images)]

    wait_blocks(out_r, n_all - 1, recv_sem.at[OUT])
    slot_out = both_halves(out_r)
    shares = []
    for b in range(images):
        dot = nt(slot_out[b], grad[b])
        shares.append(combine[b] * (dot - jnp.sum(combine[b] * dot, axis=0, keepdims=True)))
    wait_blocks(in_r, n_all - 1, recv_sem.at[IN])
    slot_in_grad = both_halves(in_r)
    for b in range(images):
        dot = nt(slot_in_grad[b], tok[b])
        shares[b] += dispatch[b] * (dot - jnp.sum(dispatch[b] * dot, axis=1, keepdims=True))
        lg_s[:, b * patches : (b + 1) * patches] = shares[b]
    swap_lg = to_partner(lg_s, lg_r, LOGIT_GRAD)
    swap_lg.start()
    swap_lg.wait()
    logit_b = (lg_s[...] + lg_r[...]).astype(BF16)

    part = nn(logit_b, tok_rows)
    rs_s[...] = part.reshape(n_ep, experts // n_ep, width)
    rs_r[ep] = rs_s[ep]
    send_row(lambda to_ep: rs_s.at[to_ep], rs_r, SCATTER)

    def tokens_of(b):
        left = jnp.concatenate([dispatch_b[b], per_image(logit_b)[b]], axis=0)
        right = jnp.concatenate([slot_in_grad[b], router_t], axis=0)
        grad_tokens_o[b] = tn(left, right).astype(BF16)

    for b in range(images // 2):
        tokens_of(b)
    wait_blocks(rs_r, n_ep - 1, recv_sem.at[SCATTER])
    ag[ep] = jnp.sum(rs_r[...], axis=0)
    send_row(lambda to_ep: ag.at[ep], ag, GATHER)
    for b in range(images // 2, images):
        tokens_of(b)
    wait_blocks(ag, n_ep - 1, recv_sem.at[GATHER])
    grad_router_o[...] = ag[...].reshape(experts, width)

    wait_blocks(slots_r, n_all - 1, send_sem.at[SLOTS])
    wait_blocks(grads_r, n_all - 1, send_sem.at[GRADS])
    wait_blocks(out_r, n_all - 1, send_sem.at[OUT])
    wait_blocks(in_r, n_all - 1, send_sem.at[IN])
    wait_blocks(rs_r, n_ep - 1, send_sem.at[SCATTER])
    wait_blocks(ag, n_ep - 1, send_sem.at[GATHER])


def write_out(tokens_v, router_v, w_v, tokens_o, router_o, w_o, sem):
    cut = w_v.shape[0] // 4
    pairs = [(w_v.at[pl.ds(i * cut, cut)], w_o.at[pl.ds(i * cut, cut)]) for i in range(4)]
    pairs += [(tokens_v, tokens_o), (router_v, router_o)]
    copies = [pltpu.make_async_copy(a, b, sem.at[i]) for i, (a, b) in enumerate(pairs)]
    for copy in copies:
        copy.start()
    for copy in copies:
        copy.wait()


def on_device(n_ep, tokens, router, w_in, w_out, grad_out):
    images, patches, width = tokens.shape
    experts = router.shape[1]
    w_in, w_out = w_in[0], w_out[0]
    model, hidden = w_in.shape
    rows = n_ep * images
    n_all = 2 * n_ep
    vmem = pltpu.VMEM
    grad_tokens, grad_router, grad_w = pl.pallas_call(
        functools.partial(kernel, n_ep),
        out_shape=(
            pltpu.VMEM(tokens.shape, BF16),
            pltpu.VMEM((experts, width), F32),
            pltpu.VMEM(w_in.shape, BF16),
        ),
        in_specs=[pl.BlockSpec(memory_space=pltpu.HBM)] * 5,
        out_specs=(pl.BlockSpec(memory_space=pltpu.VMEM),) * 3,
        scratch_shapes=[
            vmem(tokens.shape, BF16),
            vmem((experts, width), BF16),
            vmem(w_in.shape, BF16),
            vmem(w_out.shape, BF16),
            vmem(grad_out.shape, BF16),
            vmem((experts, images * patches), F32),
            vmem((experts, images * patches), F32),
            vmem((experts, images, width), BF16),
            vmem((n_all, images, width), BF16),
            vmem((experts, images, width), BF16),
            vmem((n_all, images, width), BF16),
            vmem((rows, model), BF16),
            vmem((rows, model), BF16),
            vmem((rows, hidden), BF16),
            vmem((n_all, images, width), BF16),
            vmem((n_all, images, width), BF16),
            vmem((n_all, images, width), BF16),
            vmem((n_all, images, width), BF16),
            vmem((experts, images * patches), F32),
            vmem((experts, images * patches), F32),
            vmem((n_ep, experts // n_ep, width), F32),
            vmem((n_ep, experts // n_ep, width), F32),
            vmem((n_ep, experts // n_ep, width), F32),
            pltpu.SemaphoreType.DMA((5,)),
            pltpu.SemaphoreType.DMA((8,)),
            pltpu.SemaphoreType.DMA((8,)),
        ],
        compiler_params=pltpu.CompilerParams(
            collective_id=0, has_side_effects=True, vmem_limit_bytes=40 * 1024 * 1024
        ),
    )(*(pltpu.with_memory_space_constraint(x, pltpu.HBM) for x in (tokens, router.T, w_in, w_out, grad_out)))
    results = (grad_tokens, grad_router, grad_w)
    grad_tokens, grad_router, grad_w = pl.pallas_call(
        write_out,
        out_shape=tuple(jax.ShapeDtypeStruct(x.shape, x.dtype) for x in results),
        in_specs=[pl.BlockSpec(memory_space=pltpu.VMEM)] * 3,
        out_specs=(pl.BlockSpec(memory_space=pltpu.HBM),) * 3,
        scratch_shapes=[pltpu.SemaphoreType.DMA((6,))],
        compiler_params=pltpu.CompilerParams(vmem_limit_bytes=8 * 1024 * 1024),
    )(*(pltpu.with_memory_space_constraint(x, pltpu.VMEM) for x in results))
    return grad_tokens, grad_router.T, grad_w.reshape(1, model, hidden)


def solution(mesh):
    placed = (
        P("ep", None, "tp"),
        P("tp", None),
        P("ep", None, "tp"),
        P("ep", "tp", None),
        P("ep", None, "tp"),
    )
    return jax.shard_map(
        functools.partial(on_device, mesh.shape["ep"]),
        mesh=mesh,
        in_specs=placed,
        out_specs=(P("ep", None, "tp"), P("tp", None), P("ep", None, "tp")),
        check_vma=False,
    )
```

```python
import functools

import jax
import jax.numpy as jnp
from jax import lax
from jax.experimental import pallas as pl
from jax.experimental.pallas import tpu as pltpu
from jax.sharding import PartitionSpec as P

F32 = jnp.float32
BF16 = jnp.bfloat16
MESH = pl.DeviceIdType.MESH

SLOTS, GRADS, OUT, IN, SCATTER, GATHER = range(6)
SINGLE = 6


def nt(a, b):
    return lax.dot_general(a, b, (((1,), (1,)), ((), ())), preferred_element_type=F32)


def tn(a, b):
    return lax.dot_general(a, b, (((0,), (0,)), ((), ())), preferred_element_type=F32)


def nn(a, b):
    return jnp.dot(a, b, preferred_element_type=F32)


def gelu_parts(v):
    c = 0.7978845608028654
    t = jnp.tanh(c * (v + 0.044715 * (v * v * v)))
    half = 0.5 * (1.0 + t)
    slope = half + (0.5 * c) * v * (1.0 - t * t) * (1.0 + (3.0 * 0.044715) * (v * v))
    return v * half, slope


def kernel(
    n_ep,
    tok_h, router_h, w_in_h, w_out_h, grad_h,
    grad_tokens_o, grad_router_o, grad_w_o,
    tok, router, w_in, w_out, grad,
    logits_s, logits_r, slots_s, slots_r, grads_s, grads_r, slot_in, slot_grad, pre_grad,
    out_s, out_r, in_s, in_r, lg_s, lg_r, rs_s, rs_r, ag,
    load_sem, send_sem, recv_sem,
):
    ep, tp = lax.axis_index("ep"), lax.axis_index("tp")
    other = 1 - tp
    n_all = 2 * n_ep
    me = tp * n_ep + ep
    images, patches, width = tok.shape
    experts = router.shape[0]
    rows = n_ep * images

    loads = [
        pltpu.make_async_copy(src, dst, load_sem.at[i])
        for i, (src, dst) in enumerate(
            ((tok_h, tok), (router_h, router), (grad_h, grad), (w_in_h, w_in), (w_out_h, w_out))
        )
    ]
    for load in loads:
        load.start()

    barrier = pltpu.get_barrier_semaphore()

    low = ep < n_ep // 2

    def wrapped(off):
        to = jnp.where(low, ep - off, ep + off)
        to = jnp.where(to < 0, to + n_ep, to)
        return jnp.where(to >= n_ep, to - n_ep, to)

    def others(act):
        group = next(k for k in (5, 3, 1) if (n_ep - 1) % k == 0)

        def step(i, carry):
            for j in range(group):
                act(wrapped(i * group + (j + 1)))
            return carry

        lax.fori_loop(0, (n_ep - 1) // group, step, 0)

    def greet(to_ep, to_tp):
        pl.semaphore_signal(barrier, inc=1, device_id=(to_ep, to_tp), device_id_type=MESH)

    greet(ep, other)
    others(lambda to_ep: (greet(to_ep, tp), greet(to_ep, other)))

    def to_partner(src, dst, k):
        return pltpu.make_async_remote_copy(
            src_ref=src, dst_ref=dst, send_sem=send_sem.at[k], recv_sem=recv_sem.at[k],
            device_id=(ep, other), device_id_type=MESH,
        )

    def send(src, dst, k, to_ep, to_tp):
        pltpu.make_async_remote_copy(
            src_ref=src, dst_ref=dst.at[me],
            send_sem=send_sem.at[k], recv_sem=recv_sem.at[k],
            device_id=(to_ep, to_tp), device_id_type=MESH,
        ).start()

    def send_all(src, dst, k):
        others(
            lambda to_ep: (
                send(src.at[to_ep], dst, k, to_ep, tp),
                send(src.at[to_ep], dst, k, to_ep, other),
            )
        )
        send(src.at[ep], dst, k, ep, other)

    def send_row(src, dst, k):
        def send_one(to_ep):
            pltpu.make_async_remote_copy(
                src_ref=src(to_ep), dst_ref=dst.at[ep],
                send_sem=send_sem.at[k], recv_sem=recv_sem.at[k],
                device_id=(to_ep, tp), device_id_type=MESH,
            ).start()

        others(send_one)

    def wait_blocks(ref, count, sem):
        blocks = ref.at[pl.ds(0, count)]
        pltpu.make_async_copy(blocks, blocks, sem).wait()

    loads[0].wait()
    loads[1].wait()
    router_t = router[...]
    for b in range(images):
        logits_s[b] = nt(router_t, tok[b])
    pl.semaphore_wait(barrier, n_all - 1)
    swaps = [to_partner(logits_s.at[b], logits_r.at[b], SINGLE + b) for b in range(images)]
    for swap in swaps:
        swap.start()

    def softmax(x, axis):
        e = jnp.exp(x - jnp.max(x, axis=axis, keepdims=True))
        return e / jnp.sum(e, axis=axis, keepdims=True)

    dispatch, combine = [], []
    for b in range(images):
        swaps[b].wait()
        logits = logits_s[b] + logits_r[b]
        dispatch.append(softmax(logits, 1))
        combine.append(softmax(logits, 0))
    dispatch_b = [x.astype(BF16) for x in dispatch]

    def halves(weights, rows_of, ref_s, ref_r, k):
        parts = [nn(weights[b], rows_of[b]) for b in range(images)]
        ref_s[...] = jnp.stack(parts, axis=1).astype(BF16)
        ref_r[me] = ref_s[ep]
        send_all(ref_s, ref_r, k)

    halves(dispatch_b, tok, slots_s, slots_r, SLOTS)
    loads[2].wait()
    halves([x.astype(BF16) for x in combine], grad, grads_s, grads_r, GRADS)

    def arrived(ref, dst, k):
        wait_blocks(ref, n_all - 1, recv_sem.at[k])
        for s in range(2):
            half = ref[s * n_ep : (s + 1) * n_ep].astype(F32)
            dst[:, s * width : (s + 1) * width] = half.reshape(rows, width).astype(BF16)

    loads[3].wait()
    loads[4].wait()
    arrived(slots_r, slot_in, SLOTS)

    def send_back(half_of, src, dst, k):
        for s in range(2):
            part = half_of(slice(s * width, (s + 1) * width))
            src[s * n_ep : (s + 1) * n_ep] = part.reshape(n_ep, images, width).astype(BF16)
            others(lambda to_ep: send(src.at[s * n_ep + to_ep], dst, k, to_ep, s))
        send(src.at[other * n_ep + ep], dst, k, ep, other)
        dst[me] = src[me]

    act, slope = gelu_parts(nn(slot_in[...], w_in[...]))
    act = act.astype(BF16)
    send_back(lambda cols: nn(act, w_out[:, cols]), out_s, out_r, OUT)
    arrived(grads_r, slot_grad, GRADS)
    pre_grad[...] = (slope * nt(slot_grad[...], w_out[...])).astype(BF16)
    send_back(lambda cols: nt(pre_grad[...], w_in[cols, :]), in_s, in_r, IN)

    tile = 256 if grad_w_o.shape[0] % 256 == 0 else 128

    def grad_w_tile(i, carry):
        at = pl.ds(pl.multiple_of(i * tile, tile), tile)
        grad_w_o[at, :] = tn(slot_in[:, at], pre_grad[...]).astype(BF16)
        return carry

    lax.fori_loop(0, grad_w_o.shape[0] // tile, grad_w_tile, 0)

    def both_halves(ref):
        total = ref[:n_ep].astype(F32) + ref[n_ep:].astype(F32)
        return [total[:, b, :].astype(BF16) for b in range(images)]

    wait_blocks(out_r, n_all - 1, recv_sem.at[OUT])
    slot_out = both_halves(out_r)
    shares = []
    for b in range(images):
        dot = nt(slot_out[b], grad[b])
        shares.append(combine[b] * (dot - jnp.sum(combine[b] * dot, axis=0, keepdims=True)))
    wait_blocks(in_r, n_all - 1, recv_sem.at[IN])
    slot_in_grad = both_halves(in_r)
    swaps = []
    for b in range(images):
        dot = nt(slot_in_grad[b], tok[b])
        lg_s[b] = shares[b] + dispatch[b] * (
            dot - jnp.sum(dispatch[b] * dot, axis=1, keepdims=True)
        )
        swaps.append(to_partner(lg_s.at[b], lg_r.at[b], SINGLE + images + b))
        swaps[b].start()
    logit_b, part = [], 0.0
    for b in range(images):
        swaps[b].wait()
        logit_b.append((lg_s[b] + lg_r[b]).astype(BF16))
        part += nn(logit_b[b], tok[b])

    rs_s[...] = part.reshape(n_ep, experts // n_ep, width)
    rs_r[ep] = rs_s[ep]
    send_row(lambda to_ep: rs_s.at[to_ep], rs_r, SCATTER)

    def tokens_of(b):
        left = jnp.concatenate([dispatch_b[b], logit_b[b]], axis=0)
        right = jnp.concatenate([slot_in_grad[b], router_t], axis=0)
        grad_tokens_o[b] = tn(left, right).astype(BF16)

    for b in range(images // 2):
        tokens_of(b)
    wait_blocks(rs_r, n_ep - 1, recv_sem.at[SCATTER])
    ag[ep] = jnp.sum(rs_r[...], axis=0)
    send_row(lambda to_ep: ag.at[ep], ag, GATHER)
    for b in range(images // 2, images):
        tokens_of(b)
    wait_blocks(ag, n_ep - 1, recv_sem.at[GATHER])
    grad_router_o[...] = ag[...].reshape(experts, width)

    wait_blocks(slots_r, n_all - 1, send_sem.at[SLOTS])
    wait_blocks(grads_r, n_all - 1, send_sem.at[GRADS])
    wait_blocks(out_r, n_all - 1, send_sem.at[OUT])
    wait_blocks(in_r, n_all - 1, send_sem.at[IN])
    wait_blocks(rs_r, n_ep - 1, send_sem.at[SCATTER])
    wait_blocks(ag, n_ep - 1, send_sem.at[GATHER])


def write_out(tokens_v, router_v, w_v, tokens_o, router_o, w_o, sem):
    cut = w_v.shape[0] // 4
    pairs = [(w_v.at[pl.ds(i * cut, cut)], w_o.at[pl.ds(i * cut, cut)]) for i in range(4)]
    pairs += [(tokens_v, tokens_o), (router_v, router_o)]
    copies = [pltpu.make_async_copy(a, b, sem.at[i]) for i, (a, b) in enumerate(pairs)]
    for copy in copies:
        copy.start()
    for copy in copies:
        copy.wait()


def on_device(n_ep, tokens, router, w_in, w_out, grad_out):
    images, patches, width = tokens.shape
    experts = router.shape[1]
    w_in, w_out = w_in[0], w_out[0]
    model, hidden = w_in.shape
    rows = n_ep * images
    n_all = 2 * n_ep
    vmem = pltpu.VMEM
    grad_tokens, grad_router, grad_w = pl.pallas_call(
        functools.partial(kernel, n_ep),
        out_shape=(
            pltpu.VMEM(tokens.shape, BF16),
            pltpu.VMEM((experts, width), F32),
            pltpu.VMEM(w_in.shape, BF16),
        ),
        in_specs=[pl.BlockSpec(memory_space=pltpu.HBM)] * 5,
        out_specs=(pl.BlockSpec(memory_space=pltpu.VMEM),) * 3,
        scratch_shapes=[
            vmem(tokens.shape, BF16),
            vmem((experts, width), BF16),
            vmem(w_in.shape, BF16),
            vmem(w_out.shape, BF16),
            vmem(grad_out.shape, BF16),
            vmem((images, experts, patches), F32),
            vmem((images, experts, patches), F32),
            vmem((experts, images, width), BF16),
            vmem((n_all, images, width), BF16),
            vmem((experts, images, width), BF16),
            vmem((n_all, images, width), BF16),
            vmem((rows, model), BF16),
            vmem((rows, model), BF16),
            vmem((rows, hidden), BF16),
            vmem((n_all, images, width), BF16),
            vmem((n_all, images, width), BF16),
            vmem((n_all, images, width), BF16),
            vmem((n_all, images, width), BF16),
            vmem((images, experts, patches), F32),
            vmem((images, experts, patches), F32),
            vmem((n_ep, experts // n_ep, width), F32),
            vmem((n_ep, experts // n_ep, width), F32),
            vmem((n_ep, experts // n_ep, width), F32),
            pltpu.SemaphoreType.DMA((5,)),
            pltpu.SemaphoreType.DMA((SINGLE + 2 * images,)),
            pltpu.SemaphoreType.DMA((SINGLE + 2 * images,)),
        ],
        compiler_params=pltpu.CompilerParams(
            collective_id=0, has_side_effects=True, vmem_limit_bytes=40 * 1024 * 1024
        ),
    )(*(pltpu.with_memory_space_constraint(x, pltpu.HBM) for x in (tokens, router.T, w_in, w_out, grad_out)))
    results = (grad_tokens, grad_router, grad_w)
    grad_tokens, grad_router, grad_w = pl.pallas_call(
        write_out,
        out_shape=tuple(jax.ShapeDtypeStruct(x.shape, x.dtype) for x in results),
        in_specs=[pl.BlockSpec(memory_space=pltpu.VMEM)] * 3,
        out_specs=(pl.BlockSpec(memory_space=pltpu.HBM),) * 3,
        scratch_shapes=[pltpu.SemaphoreType.DMA((6,))],
        compiler_params=pltpu.CompilerParams(vmem_limit_bytes=8 * 1024 * 1024),
    )(*(pltpu.with_memory_space_constraint(x, pltpu.VMEM) for x in results))
    return grad_tokens, grad_router.T, grad_w.reshape(1, model, hidden)


def solution(mesh):
    placed = (
        P("ep", None, "tp"),
        P("tp", None),
        P("ep", None, "tp"),
        P("ep", "tp", None),
        P("ep", None, "tp"),
    )
    return jax.shard_map(
        functools.partial(on_device, mesh.shape["ep"]),
        mesh=mesh,
        in_specs=placed,
        out_specs=(P("ep", None, "tp"), P("tp", None), P("ep", None, "tp")),
        check_vma=False,
    )
```

```python
import functools

import jax
import jax.numpy as jnp
from jax import lax
from jax.experimental import pallas as pl
from jax.experimental.pallas import tpu as pltpu
from jax.sharding import PartitionSpec as P

F32 = jnp.float32
BF16 = jnp.bfloat16
MESH = pl.DeviceIdType.MESH

SLOTS, GRADS, BACK, SCATTER, GATHER = range(5)
SINGLE = 5


def nt(a, b):
    return lax.dot_general(a, b, (((1,), (1,)), ((), ())), preferred_element_type=F32)


def tn(a, b):
    return lax.dot_general(a, b, (((0,), (0,)), ((), ())), preferred_element_type=F32)


def nn(a, b):
    return jnp.dot(a, b, preferred_element_type=F32)


def gelu_parts(v):
    c = 0.7978845608028654
    t = jnp.tanh(c * (v + 0.044715 * (v * v * v)))
    half = 0.5 * (1.0 + t)
    slope = half + (0.5 * c) * v * (1.0 - t * t) * (1.0 + (3.0 * 0.044715) * (v * v))
    return v * half, slope


def kernel(
    n_ep,
    tok_h, router_h, w_in_h, w_out_h, grad_h,
    grad_tokens_o, grad_router_o, grad_w_o,
    tok, router, w_in, w_out, grad,
    logits_s, logits_r, slots_s, slots_r, grads_s, grads_r, slot_in, slot_grad, pre_grad,
    back_s, back_r, lg_s, lg_r, rs_s, rs_r, ag,
    load_sem, send_sem, recv_sem,
):
    ep, tp = lax.axis_index("ep"), lax.axis_index("tp")
    other = 1 - tp
    n_all = 2 * n_ep
    me = tp * n_ep + ep
    images, patches, width = tok.shape
    experts = router.shape[0]
    rows = n_ep * images

    loads = [
        pltpu.make_async_copy(src, dst, load_sem.at[i])
        for i, (src, dst) in enumerate(
            ((tok_h, tok), (router_h, router), (grad_h, grad), (w_in_h, w_in), (w_out_h, w_out))
        )
    ]
    for load in loads:
        load.start()

    barrier = pltpu.get_barrier_semaphore()

    low = ep < n_ep // 2

    def wrapped(off):
        to = jnp.where(low, ep - off, ep + off)
        to = jnp.where(to < 0, to + n_ep, to)
        return jnp.where(to >= n_ep, to - n_ep, to)

    def others(act):
        group = next(k for k in (5, 3, 1) if (n_ep - 1) % k == 0)

        def step(i, carry):
            for j in range(group):
                act(wrapped(i * group + (j + 1)))
            return carry

        lax.fori_loop(0, (n_ep - 1) // group, step, 0)

    def greet(to_ep, to_tp):
        pl.semaphore_signal(barrier, inc=1, device_id=(to_ep, to_tp), device_id_type=MESH)

    greet(ep, other)
    others(lambda to_ep: (greet(to_ep, tp), greet(to_ep, other)))

    def to_partner(src, dst, k):
        return pltpu.make_async_remote_copy(
            src_ref=src, dst_ref=dst, send_sem=send_sem.at[k], recv_sem=recv_sem.at[k],
            device_id=(ep, other), device_id_type=MESH,
        )

    def send(src, dst, k, to_ep, to_tp):
        pltpu.make_async_remote_copy(
            src_ref=src, dst_ref=dst.at[me],
            send_sem=send_sem.at[k], recv_sem=recv_sem.at[k],
            device_id=(to_ep, to_tp), device_id_type=MESH,
        ).start()

    def send_all(src, dst, k):
        others(
            lambda to_ep: (
                send(src.at[to_ep], dst, k, to_ep, tp),
                send(src.at[to_ep], dst, k, to_ep, other),
            )
        )
        send(src.at[ep], dst, k, ep, other)

    def send_row(src, dst, k):
        def send_one(to_ep):
            pltpu.make_async_remote_copy(
                src_ref=src(to_ep), dst_ref=dst.at[ep],
                send_sem=send_sem.at[k], recv_sem=recv_sem.at[k],
                device_id=(to_ep, tp), device_id_type=MESH,
            ).start()

        others(send_one)

    def wait_blocks(ref, count, sem):
        blocks = ref.at[pl.ds(0, count)]
        pltpu.make_async_copy(blocks, blocks, sem).wait()

    loads[0].wait()
    loads[1].wait()
    router_t = router[...]
    for b in range(images):
        logits_s[b] = nt(router_t, tok[b])
    pl.semaphore_wait(barrier, n_all - 1)
    swaps = [to_partner(logits_s.at[b], logits_r.at[b], SINGLE + b) for b in range(images)]
    for swap in swaps:
        swap.start()

    def softmax(x, axis):
        e = jnp.exp(x - jnp.max(x, axis=axis, keepdims=True))
        return e / jnp.sum(e, axis=axis, keepdims=True)

    dispatch, combine = [], []
    for b in range(images):
        swaps[b].wait()
        logits = logits_s[b] + logits_r[b]
        dispatch.append(softmax(logits, 1))
        combine.append(softmax(logits, 0))
    dispatch_b = [x.astype(BF16) for x in dispatch]

    def halves(weights, rows_of, ref_s, ref_r, k):
        parts = [nn(weights[b], rows_of[b]) for b in range(images)]
        ref_s[...] = jnp.stack(parts, axis=1).astype(BF16)
        ref_r[me] = ref_s[ep]
        send_all(ref_s, ref_r, k)

    halves(dispatch_b, tok, slots_s, slots_r, SLOTS)
    loads[2].wait()
    halves([x.astype(BF16) for x in combine], grad, grads_s, grads_r, GRADS)

    def arrived(ref, dst, k):
        wait_blocks(ref, n_all - 1, recv_sem.at[k])
        for s in range(2):
            half = ref[s * n_ep : (s + 1) * n_ep].astype(F32)
            dst[:, s * width : (s + 1) * width] = half.reshape(rows, width).astype(BF16)

    loads[3].wait()
    loads[4].wait()
    arrived(slots_r, slot_in, SLOTS)

    act, slope = gelu_parts(nn(slot_in[...], w_in[...]))
    arrived(grads_r, slot_grad, GRADS)
    pre_grad[...] = (slope * nt(slot_grad[...], w_out[...])).astype(BF16)
    parts = (nt(pre_grad[...], w_in[...]), nn(act.astype(BF16), w_out[...]))
    for s in range(2):
        cut = [x[:, s * width : (s + 1) * width].reshape(n_ep, images, width) for x in parts]
        back_s[s * n_ep : (s + 1) * n_ep] = jnp.concatenate(cut, axis=1).astype(BF16)
    back_r[me] = back_s[me]
    others(
        lambda to_ep: (
            send(back_s.at[tp * n_ep + to_ep], back_r, BACK, to_ep, tp),
            send(back_s.at[other * n_ep + to_ep], back_r, BACK, to_ep, other),
        )
    )
    send(back_s.at[other * n_ep + ep], back_r, BACK, ep, other)

    tile = 256 if grad_w_o.shape[0] % 256 == 0 else 128

    def grad_w_tile(i, carry):
        at = pl.ds(pl.multiple_of(i * tile, tile), tile)
        grad_w_o[at, :] = tn(slot_in[:, at], pre_grad[...]).astype(BF16)
        return carry

    lax.fori_loop(0, grad_w_o.shape[0] // tile, grad_w_tile, 0)

    wait_blocks(back_r, n_all - 1, recv_sem.at[BACK])
    total = back_r[:n_ep].astype(F32) + back_r[n_ep:].astype(F32)
    slot_in_grad = [total[:, b, :].astype(BF16) for b in range(images)]
    slot_out = [total[:, images + b, :].astype(BF16) for b in range(images)]
    swaps = []
    for b in range(images):
        dot = nt(slot_out[b], grad[b])
        share = combine[b] * (dot - jnp.sum(combine[b] * dot, axis=0, keepdims=True))
        dot = nt(slot_in_grad[b], tok[b])
        lg_s[b] = share + dispatch[b] * (
            dot - jnp.sum(dispatch[b] * dot, axis=1, keepdims=True)
        )
        swaps.append(to_partner(lg_s.at[b], lg_r.at[b], SINGLE + images + b))
        swaps[b].start()
    logit_b, part = [], 0.0
    for b in range(images):
        swaps[b].wait()
        logit_b.append((lg_s[b] + lg_r[b]).astype(BF16))
        part += nn(logit_b[b], tok[b])

    rs_s[...] = part.reshape(n_ep, experts // n_ep, width)
    rs_r[ep] = rs_s[ep]
    send_row(lambda to_ep: rs_s.at[to_ep], rs_r, SCATTER)

    def tokens_of(b):
        left = jnp.concatenate([dispatch_b[b], logit_b[b]], axis=0)
        right = jnp.concatenate([slot_in_grad[b], router_t], axis=0)
        grad_tokens_o[b] = tn(left, right).astype(BF16)

    for b in range(images // 2):
        tokens_of(b)
    wait_blocks(rs_r, n_ep - 1, recv_sem.at[SCATTER])
    ag[ep] = jnp.sum(rs_r[...], axis=0)
    send_row(lambda to_ep: ag.at[ep], ag, GATHER)
    for b in range(images // 2, images):
        tokens_of(b)
    wait_blocks(ag, n_ep - 1, recv_sem.at[GATHER])
    grad_router_o[...] = ag[...].reshape(experts, width)

    wait_blocks(slots_r, n_all - 1, send_sem.at[SLOTS])
    wait_blocks(grads_r, n_all - 1, send_sem.at[GRADS])
    wait_blocks(back_r, n_all - 1, send_sem.at[BACK])
    wait_blocks(rs_r, n_ep - 1, send_sem.at[SCATTER])
    wait_blocks(ag, n_ep - 1, send_sem.at[GATHER])


def write_out(tokens_v, router_v, w_v, tokens_o, router_o, w_o, sem):
    cut = w_v.shape[0] // 4
    pairs = [(w_v.at[pl.ds(i * cut, cut)], w_o.at[pl.ds(i * cut, cut)]) for i in range(4)]
    pairs += [(tokens_v, tokens_o), (router_v, router_o)]
    copies = [pltpu.make_async_copy(a, b, sem.at[i]) for i, (a, b) in enumerate(pairs)]
    for copy in copies:
        copy.start()
    for copy in copies:
        copy.wait()


def on_device(n_ep, tokens, router, w_in, w_out, grad_out):
    images, patches, width = tokens.shape
    experts = router.shape[1]
    w_in, w_out = w_in[0], w_out[0]
    model, hidden = w_in.shape
    rows = n_ep * images
    n_all = 2 * n_ep
    vmem = pltpu.VMEM
    grad_tokens, grad_router, grad_w = pl.pallas_call(
        functools.partial(kernel, n_ep),
        out_shape=(
            pltpu.VMEM(tokens.shape, BF16),
            pltpu.VMEM((experts, width), F32),
            pltpu.VMEM(w_in.shape, BF16),
        ),
        in_specs=[pl.BlockSpec(memory_space=pltpu.HBM)] * 5,
        out_specs=(pl.BlockSpec(memory_space=pltpu.VMEM),) * 3,
        scratch_shapes=[
            vmem(tokens.shape, BF16),
            vmem((experts, width), BF16),
            vmem(w_in.shape, BF16),
            vmem(w_out.shape, BF16),
            vmem(grad_out.shape, BF16),
            vmem((images, experts, patches), F32),
            vmem((images, experts, patches), F32),
            vmem((experts, images, width), BF16),
            vmem((n_all, images, width), BF16),
            vmem((experts, images, width), BF16),
            vmem((n_all, images, width), BF16),
            vmem((rows, model), BF16),
            vmem((rows, model), BF16),
            vmem((rows, hidden), BF16),
            vmem((n_all, 2 * images, width), BF16),
            vmem((n_all, 2 * images, width), BF16),
            vmem((images, experts, patches), F32),
            vmem((images, experts, patches), F32),
            vmem((n_ep, experts // n_ep, width), F32),
            vmem((n_ep, experts // n_ep, width), F32),
            vmem((n_ep, experts // n_ep, width), F32),
            pltpu.SemaphoreType.DMA((5,)),
            pltpu.SemaphoreType.DMA((SINGLE + 2 * images,)),
            pltpu.SemaphoreType.DMA((SINGLE + 2 * images,)),
        ],
        compiler_params=pltpu.CompilerParams(
            collective_id=0, has_side_effects=True, vmem_limit_bytes=40 * 1024 * 1024
        ),
    )(*(pltpu.with_memory_space_constraint(x, pltpu.HBM) for x in (tokens, router.T, w_in, w_out, grad_out)))
    results = (grad_tokens, grad_router, grad_w)
    grad_tokens, grad_router, grad_w = pl.pallas_call(
        write_out,
        out_shape=tuple(jax.ShapeDtypeStruct(x.shape, x.dtype) for x in results),
        in_specs=[pl.BlockSpec(memory_space=pltpu.VMEM)] * 3,
        out_specs=(pl.BlockSpec(memory_space=pltpu.HBM),) * 3,
        scratch_shapes=[pltpu.SemaphoreType.DMA((6,))],
        compiler_params=pltpu.CompilerParams(vmem_limit_bytes=8 * 1024 * 1024),
    )(*(pltpu.with_memory_space_constraint(x, pltpu.VMEM) for x in results))
    return grad_tokens, grad_router.T, grad_w.reshape(1, model, hidden)


def solution(mesh):
    placed = (
        P("ep", None, "tp"),
        P("tp", None),
        P("ep", None, "tp"),
        P("ep", "tp", None),
        P("ep", None, "tp"),
    )
    return jax.shard_map(
        functools.partial(on_device, mesh.shape["ep"]),
        mesh=mesh,
        in_specs=placed,
        out_specs=(P("ep", None, "tp"), P("tp", None), P("ep", None, "tp")),
        check_vma=False,
    )
```

```python
import functools

import jax
import jax.numpy as jnp
from jax import lax
from jax.experimental import pallas as pl
from jax.experimental.pallas import tpu as pltpu
from jax.sharding import PartitionSpec as P

F32 = jnp.float32
BF16 = jnp.bfloat16
MESH = pl.DeviceIdType.MESH

SLOTS, GRADS, OUT, IN, SCATTER, GATHER, SINGLE = 0, 2, 3, 4, 5, 6, 7


def nt(a, b):
    return lax.dot_general(a, b, (((1,), (1,)), ((), ())), preferred_element_type=F32)


def tn(a, b):
    return lax.dot_general(a, b, (((0,), (0,)), ((), ())), preferred_element_type=F32)


def nn(a, b):
    return jnp.dot(a, b, preferred_element_type=F32)


def gelu_parts(v):
    c = 0.7978845608028654
    t = jnp.tanh(c * (v + 0.044715 * (v * v * v)))
    half = 0.5 * (1.0 + t)
    slope = half + (0.5 * c) * v * (1.0 - t * t) * (1.0 + (3.0 * 0.044715) * (v * v))
    return v * half, slope


def kernel(
    n_ep,
    tok_h, router_h, w_in_h, w_out_h, grad_h,
    grad_tokens_o, grad_router_o, grad_w_o,
    tok, router, w_in, w_out, grad,
    logits_s, logits_r, slots_s, slots_r, grads_s, grads_r, slot_in, slot_grad, pre_grad,
    out_s, out_r, in_s, in_r, lg_s, lg_r, rs_s, rs_r, ag,
    load_sem, send_sem, recv_sem,
):
    ep, tp = lax.axis_index("ep"), lax.axis_index("tp")
    other = 1 - tp
    n_all = 2 * n_ep
    me = tp * n_ep + ep
    images, patches, width = tok.shape
    experts = router.shape[0]
    rows = n_ep * images

    loads = [
        pltpu.make_async_copy(src, dst, load_sem.at[i])
        for i, (src, dst) in enumerate(
            ((tok_h, tok), (router_h, router), (grad_h, grad), (w_in_h, w_in), (w_out_h, w_out))
        )
    ]
    loads[0].start()
    loads[1].start()

    barrier = pltpu.get_barrier_semaphore()

    low = ep < n_ep // 2

    def wrapped(off):
        to = jnp.where(low, ep - off, ep + off)
        to = jnp.where(to < 0, to + n_ep, to)
        return jnp.where(to >= n_ep, to - n_ep, to)

    def others(act):
        group = next(k for k in (5, 3, 1) if (n_ep - 1) % k == 0)

        def step(i, carry):
            for j in range(group):
                act(wrapped(i * group + (j + 1)))
            return carry

        lax.fori_loop(0, (n_ep - 1) // group, step, 0)

    def greet(to_ep, to_tp):
        pl.semaphore_signal(barrier, inc=1, device_id=(to_ep, to_tp), device_id_type=MESH)

    greet(ep, other)
    others(lambda to_ep: (greet(to_ep, tp), greet(to_ep, other)))
    for load in loads[2:]:
        load.start()

    def to_partner(src, dst, k):
        return pltpu.make_async_remote_copy(
            src_ref=src, dst_ref=dst, send_sem=send_sem.at[k], recv_sem=recv_sem.at[k],
            device_id=(ep, other), device_id_type=MESH,
        )

    def send(src, dst, k, to_ep, to_tp):
        pltpu.make_async_remote_copy(
            src_ref=src, dst_ref=dst.at[me],
            send_sem=send_sem.at[k], recv_sem=recv_sem.at[k],
            device_id=(to_ep, to_tp), device_id_type=MESH,
        ).start()

    def send_all(src, dst, k):
        others(
            lambda to_ep: (
                send(src.at[to_ep], dst, k, to_ep, tp),
                send(src.at[to_ep], dst, k, to_ep, other),
            )
        )
        send(src.at[ep], dst, k, ep, other)

    def send_row(src, dst, k):
        def send_one(to_ep):
            pltpu.make_async_remote_copy(
                src_ref=src(to_ep), dst_ref=dst.at[ep],
                send_sem=send_sem.at[k], recv_sem=recv_sem.at[k],
                device_id=(to_ep, tp), device_id_type=MESH,
            ).start()

        others(send_one)

    def wait_blocks(ref, count, sem):
        blocks = ref.at[pl.ds(0, count)]
        pltpu.make_async_copy(blocks, blocks, sem).wait()

    loads[0].wait()
    loads[1].wait()
    router_t = router[...]
    for b in range(images):
        logits_s[b] = nt(router_t, tok[b])
    pl.semaphore_wait(barrier, n_all - 1)
    swaps = [to_partner(logits_s.at[b], logits_r.at[b], SINGLE + b) for b in range(images)]
    for swap in swaps:
        swap.start()

    def softmax(x, axis):
        e = jnp.exp(x - jnp.max(x, axis=axis, keepdims=True))
        return e / jnp.sum(e, axis=axis, keepdims=True)

    dispatch, logits = [], []
    for b in range(images):
        swaps[b].wait()
        logits.append(logits_s[b] + logits_r[b])
        dispatch.append(softmax(logits[b], 1))
    dispatch_b = [x.astype(BF16) for x in dispatch]

    def halves(weights, rows_of, ref_s, ref_r):
        parts = [nn(weights[b], rows_of[b]) for b in range(images)]
        ref_s[...] = jnp.stack(parts, axis=1).astype(BF16)
        ref_r[me] = ref_s[ep]

    halves(dispatch_b, tok, slots_s, slots_r)
    others(lambda to_ep: send(slots_s.at[to_ep], slots_r, SLOTS + tp, to_ep, tp))
    others(lambda to_ep: send(slots_s.at[to_ep], slots_r, SLOTS + tp, to_ep, other))
    send(slots_s.at[ep], slots_r, SLOTS + tp, ep, other)
    combine = [softmax(x, 0) for x in logits]
    loads[2].wait()
    halves([x.astype(BF16) for x in combine], grad, grads_s, grads_r)
    send_all(grads_s, grads_r, GRADS)

    def arrived(ref, dst, k):
        wait_blocks(ref, n_all - 1, recv_sem.at[k])
        for s in range(2):
            half = ref[s * n_ep : (s + 1) * n_ep].astype(F32)
            dst[:, s * width : (s + 1) * width] = half.reshape(rows, width).astype(BF16)

    loads[3].wait()
    loads[4].wait()
    pre = 0.0
    for s, count in ((tp, n_ep - 1), (other, n_ep)):
        wait_blocks(slots_r, count, recv_sem.at[SLOTS + s])
        half = slots_r[pl.ds(s * n_ep, n_ep)].astype(F32).reshape(rows, width).astype(BF16)
        at = pl.ds(pl.multiple_of(s * width, 128), width)
        slot_in[:, at] = half
        pre += nn(half, w_in[at, :])

    def send_back(half_of, src, dst, k):
        for s in range(2):
            part = half_of(slice(s * width, (s + 1) * width))
            src[s * n_ep : (s + 1) * n_ep] = part.reshape(n_ep, images, width).astype(BF16)
            others(lambda to_ep: send(src.at[s * n_ep + to_ep], dst, k, to_ep, s))
        send(src.at[other * n_ep + ep], dst, k, ep, other)
        dst[me] = src[me]

    act, slope = gelu_parts(pre)
    act = act.astype(BF16)
    send_back(lambda cols: nn(act, w_out[:, cols]), out_s, out_r, OUT)
    arrived(grads_r, slot_grad, GRADS)
    pre_grad[...] = (slope * nt(slot_grad[...], w_out[...])).astype(BF16)
    send_back(lambda cols: nt(pre_grad[...], w_in[cols, :]), in_s, in_r, IN)

    tile = 256 if grad_w_o.shape[0] % 256 == 0 else 128

    def grad_w_tile(i, carry):
        at = pl.ds(pl.multiple_of(i * tile, tile), tile)
        grad_w_o[at, :] = tn(slot_in[:, at], pre_grad[...]).astype(BF16)
        return carry

    lax.fori_loop(0, grad_w_o.shape[0] // tile, grad_w_tile, 0)

    def both_halves(ref):
        total = ref[:n_ep].astype(F32) + ref[n_ep:].astype(F32)
        return [total[:, b, :].astype(BF16) for b in range(images)]

    wait_blocks(out_r, n_all - 1, recv_sem.at[OUT])
    slot_out = both_halves(out_r)
    shares = []
    for b in range(images):
        dot = nt(slot_out[b], grad[b])
        shares.append(combine[b] * (dot - jnp.sum(combine[b] * dot, axis=0, keepdims=True)))
    wait_blocks(in_r, n_all - 1, recv_sem.at[IN])
    slot_in_grad = both_halves(in_r)
    swaps = []
    for b in range(images):
        dot = nt(slot_in_grad[b], tok[b])
        lg_s[b] = shares[b] + dispatch[b] * (
            dot - jnp.sum(dispatch[b] * dot, axis=1, keepdims=True)
        )
        swaps.append(to_partner(lg_s.at[b], lg_r.at[b], SINGLE + images + b))
        swaps[b].start()
    logit_b, part = [], 0.0
    for b in range(images):
        swaps[b].wait()
        logit_b.append((lg_s[b] + lg_r[b]).astype(BF16))
        part += nn(logit_b[b], tok[b])

    rs_s[...] = part.reshape(n_ep, experts // n_ep, width)
    rs_r[ep] = rs_s[ep]
    send_row(lambda to_ep: rs_s.at[to_ep], rs_r, SCATTER)

    def tokens_of(b):
        left = jnp.concatenate([dispatch_b[b], logit_b[b]], axis=0)
        right = jnp.concatenate([slot_in_grad[b], router_t], axis=0)
        grad_tokens_o[b] = tn(left, right).astype(BF16)

    for b in range(images // 2):
        tokens_of(b)
    wait_blocks(rs_r, n_ep - 1, recv_sem.at[SCATTER])
    ag[ep] = jnp.sum(rs_r[...], axis=0)
    send_row(lambda to_ep: ag.at[ep], ag, GATHER)
    for b in range(images // 2, images):
        tokens_of(b)
    wait_blocks(ag, n_ep - 1, recv_sem.at[GATHER])
    grad_router_o[...] = ag[...].reshape(experts, width)

    wait_blocks(slots_r, n_all - 1, send_sem.at[SLOTS + tp])
    wait_blocks(grads_r, n_all - 1, send_sem.at[GRADS])
    wait_blocks(out_r, n_all - 1, send_sem.at[OUT])
    wait_blocks(in_r, n_all - 1, send_sem.at[IN])
    wait_blocks(rs_r, n_ep - 1, send_sem.at[SCATTER])
    wait_blocks(ag, n_ep - 1, send_sem.at[GATHER])


def write_out(tokens_v, router_v, w_v, tokens_o, router_o, w_o, sem):
    cut = w_v.shape[0] // 4
    pairs = [(w_v.at[pl.ds(i * cut, cut)], w_o.at[pl.ds(i * cut, cut)]) for i in range(4)]
    pairs += [(tokens_v, tokens_o), (router_v, router_o)]
    copies = [pltpu.make_async_copy(a, b, sem.at[i]) for i, (a, b) in enumerate(pairs)]
    for copy in copies:
        copy.start()
    for copy in copies:
        copy.wait()


def on_device(n_ep, tokens, router, w_in, w_out, grad_out):
    images, patches, width = tokens.shape
    experts = router.shape[1]
    w_in, w_out = w_in[0], w_out[0]
    model, hidden = w_in.shape
    rows = n_ep * images
    n_all = 2 * n_ep
    vmem = pltpu.VMEM
    grad_tokens, grad_router, grad_w = pl.pallas_call(
        functools.partial(kernel, n_ep),
        out_shape=(
            pltpu.VMEM(tokens.shape, BF16),
            pltpu.VMEM((experts, width), F32),
            pltpu.VMEM(w_in.shape, BF16),
        ),
        in_specs=[pl.BlockSpec(memory_space=pltpu.HBM)] * 5,
        out_specs=(pl.BlockSpec(memory_space=pltpu.VMEM),) * 3,
        scratch_shapes=[
            vmem(tokens.shape, BF16),
            vmem((experts, width), BF16),
            vmem(w_in.shape, BF16),
            vmem(w_out.shape, BF16),
            vmem(grad_out.shape, BF16),
            vmem((images, experts, patches), F32),
            vmem((images, experts, patches), F32),
            vmem((experts, images, width), BF16),
            vmem((n_all, images, width), BF16),
            vmem((experts, images, width), BF16),
            vmem((n_all, images, width), BF16),
            vmem((rows, model), BF16),
            vmem((rows, model), BF16),
            vmem((rows, hidden), BF16),
            vmem((n_all, images, width), BF16),
            vmem((n_all, images, width), BF16),
            vmem((n_all, images, width), BF16),
            vmem((n_all, images, width), BF16),
            vmem((images, experts, patches), F32),
            vmem((images, experts, patches), F32),
            vmem((n_ep, experts // n_ep, width), F32),
            vmem((n_ep, experts // n_ep, width), F32),
            vmem((n_ep, experts // n_ep, width), F32),
            pltpu.SemaphoreType.DMA((5,)),
            pltpu.SemaphoreType.DMA((SINGLE + 2 * images,)),
            pltpu.SemaphoreType.DMA((SINGLE + 2 * images,)),
        ],
        compiler_params=pltpu.CompilerParams(
            collective_id=0, has_side_effects=True, vmem_limit_bytes=40 * 1024 * 1024
        ),
    )(*(pltpu.with_memory_space_constraint(x, pltpu.HBM) for x in (tokens, router.T, w_in, w_out, grad_out)))
    results = (grad_tokens, grad_router, grad_w)
    grad_tokens, grad_router, grad_w = pl.pallas_call(
        write_out,
        out_shape=tuple(jax.ShapeDtypeStruct(x.shape, x.dtype) for x in results),
        in_specs=[pl.BlockSpec(memory_space=pltpu.VMEM)] * 3,
        out_specs=(pl.BlockSpec(memory_space=pltpu.HBM),) * 3,
        scratch_shapes=[pltpu.SemaphoreType.DMA((6,))],
        compiler_params=pltpu.CompilerParams(vmem_limit_bytes=8 * 1024 * 1024),
    )(*(pltpu.with_memory_space_constraint(x, pltpu.VMEM) for x in results))
    return grad_tokens, grad_router.T, grad_w.reshape(1, model, hidden)


def solution(mesh):
    placed = (
        P("ep", None, "tp"),
        P("tp", None),
        P("ep", None, "tp"),
        P("ep", "tp", None),
        P("ep", None, "tp"),
    )
    return jax.shard_map(
        functools.partial(on_device, mesh.shape["ep"]),
        mesh=mesh,
        in_specs=placed,
        out_specs=(P("ep", None, "tp"), P("tp", None), P("ep", None, "tp")),
        check_vma=False,
    )
```

```python
import functools

import jax
import jax.numpy as jnp
from jax import lax
from jax.experimental import pallas as pl
from jax.experimental.pallas import tpu as pltpu
from jax.sharding import PartitionSpec as P

F32 = jnp.float32
BF16 = jnp.bfloat16
MESH = pl.DeviceIdType.MESH

SLOTS, GRADS, OUT, IN, SCATTER, GATHER = range(6)
SINGLE = 6


def nt(a, b):
    return lax.dot_general(a, b, (((1,), (1,)), ((), ())), preferred_element_type=F32)


def tn(a, b):
    return lax.dot_general(a, b, (((0,), (0,)), ((), ())), preferred_element_type=F32)


def nn(a, b):
    return jnp.dot(a, b, preferred_element_type=F32)


def gelu_parts(v):
    c = 0.7978845608028654
    t = jnp.tanh(c * (v + 0.044715 * (v * v * v)))
    half = 0.5 * (1.0 + t)
    slope = half + (0.5 * c) * v * (1.0 - t * t) * (1.0 + (3.0 * 0.044715) * (v * v))
    return v * half, slope


def kernel(
    n_ep,
    tok_h, router_h, w_in_h, w_out_h, grad_h,
    grad_tokens_o, grad_router_o, grad_w_o,
    tok, router, w_in, w_out, grad,
    logits_s, logits_r, slots_s, slots_r, grads_s, grads_r, slot_in, slot_grad, pre_grad, act, slope, part,
    out_s, out_r, in_s, in_r, lg_s, lg_r, rs_s, rs_r, ag,
    load_sem, send_sem, recv_sem,
):
    ep, tp = lax.axis_index("ep"), lax.axis_index("tp")
    other = 1 - tp
    n_all = 2 * n_ep
    me = tp * n_ep + ep
    images, patches, width = tok.shape
    experts = router.shape[0]
    rows = n_ep * images

    loads = [
        pltpu.make_async_copy(src, dst, load_sem.at[i])
        for i, (src, dst) in enumerate(
            ((tok_h, tok), (router_h, router), (grad_h, grad), (w_in_h, w_in), (w_out_h, w_out))
        )
    ]
    for load in loads:
        load.start()

    barrier = pltpu.get_barrier_semaphore()

    low = ep < n_ep // 2

    def wrapped(off):
        to = jnp.where(low, ep - off, ep + off)
        to = jnp.where(to < 0, to + n_ep, to)
        return jnp.where(to >= n_ep, to - n_ep, to)

    def others(act):
        group = next(k for k in (5, 3, 1) if (n_ep - 1) % k == 0)

        def step(i, carry):
            for j in range(group):
                act(wrapped(i * group + (j + 1)))
            return carry

        lax.fori_loop(0, (n_ep - 1) // group, step, 0)

    def greet(to_ep, to_tp):
        pl.semaphore_signal(barrier, inc=1, device_id=(to_ep, to_tp), device_id_type=MESH)

    greet(ep, other)
    others(lambda to_ep: (greet(to_ep, tp), greet(to_ep, other)))

    def to_partner(src, dst, k):
        return pltpu.make_async_remote_copy(
            src_ref=src, dst_ref=dst, send_sem=send_sem.at[k], recv_sem=recv_sem.at[k],
            device_id=(ep, other), device_id_type=MESH,
        )

    def send(src, dst, k, to_ep, to_tp):
        pltpu.make_async_remote_copy(
            src_ref=src, dst_ref=dst.at[me],
            send_sem=send_sem.at[k], recv_sem=recv_sem.at[k],
            device_id=(to_ep, to_tp), device_id_type=MESH,
        ).start()

    def send_all(src, dst, k):
        others(
            lambda to_ep: (
                send(src.at[to_ep], dst, k, to_ep, tp),
                send(src.at[to_ep], dst, k, to_ep, other),
            )
        )
        send(src.at[ep], dst, k, ep, other)

    def send_row(src, dst, k):
        def send_one(to_ep):
            pltpu.make_async_remote_copy(
                src_ref=src(to_ep), dst_ref=dst.at[ep],
                send_sem=send_sem.at[k], recv_sem=recv_sem.at[k],
                device_id=(to_ep, tp), device_id_type=MESH,
            ).start()

        others(send_one)

    def wait_blocks(ref, count, sem):
        blocks = ref.at[pl.ds(0, count)]
        pltpu.make_async_copy(blocks, blocks, sem).wait()

    loads[0].wait()
    loads[1].wait()
    router_t = router[...]
    for b in range(images):
        logits_s[b] = nt(router_t, tok[b])
    pl.semaphore_wait(barrier, n_all - 1)
    swaps = [to_partner(logits_s.at[b], logits_r.at[b], SINGLE + b) for b in range(images)]
    for swap in swaps:
        swap.start()

    def softmax(x, axis):
        e = jnp.exp(x - jnp.max(x, axis=axis, keepdims=True))
        return e / jnp.sum(e, axis=axis, keepdims=True)

    dispatch, combine = [], []
    for b in range(images):
        swaps[b].wait()
        logits = logits_s[b] + logits_r[b]
        dispatch.append(softmax(logits, 1))
        combine.append(softmax(logits, 0))
    dispatch_b = [x.astype(BF16) for x in dispatch]

    def halves(weights, rows_of, ref_s, ref_r, k):
        parts = [nn(weights[b], rows_of[b]) for b in range(images)]
        ref_s[...] = jnp.stack(parts, axis=1).astype(BF16)
        ref_r[me] = ref_s[ep]
        send_all(ref_s, ref_r, k)

    halves(dispatch_b, tok, slots_s, slots_r, SLOTS)
    loads[2].wait()
    halves([x.astype(BF16) for x in combine], grad, grads_s, grads_r, GRADS)

    def arrived(ref, dst, k):
        wait_blocks(ref, n_all - 1, recv_sem.at[k])
        for s in range(2):
            half = ref[s * n_ep : (s + 1) * n_ep].astype(F32)
            dst[:, s * width : (s + 1) * width] = half.reshape(rows, width).astype(BF16)

    loads[3].wait()
    loads[4].wait()
    arrived(slots_r, slot_in, SLOTS)

    hidden = w_in.shape[1]
    step = 256 if hidden % 256 == 0 else 128

    def tiles(size, body):
        def one(i, carry):
            body(pl.ds(pl.multiple_of(i * step, step), step))
            return carry

        lax.fori_loop(0, size // step, one, 0)

    def send_back(half_of, src, dst, k):
        for s in range(2):
            part = half_of(slice(s * width, (s + 1) * width))
            src[s * n_ep : (s + 1) * n_ep] = part.reshape(n_ep, images, width).astype(BF16)
            others(lambda to_ep: send(src.at[s * n_ep + to_ep], dst, k, to_ep, s))
        send(src.at[other * n_ep + ep], dst, k, ep, other)
        dst[me] = src[me]

    def first(cols):
        act[:, cols], slope[:, cols] = (
            lambda a, g: (a.astype(BF16), g)
        )(*gelu_parts(nn(slot_in[...], w_in[:, cols])))

    def second(cols):
        part[:, cols] = nn(act[...], w_out[:, cols])

    def third(cols):
        back = nt(slot_grad[...], w_out[cols, :])
        pre_grad[:, cols] = (slope[:, cols] * back).astype(BF16)

    def fourth(cols):
        part[:, cols] = nt(pre_grad[...], w_in[cols, :])

    tiles(hidden, first)
    tiles(2 * width, second)
    send_back(lambda cols: part[:, cols], out_s, out_r, OUT)
    arrived(grads_r, slot_grad, GRADS)
    tiles(hidden, third)
    tiles(2 * width, fourth)
    send_back(lambda cols: part[:, cols], in_s, in_r, IN)

    tile = 256 if grad_w_o.shape[0] % 256 == 0 else 128

    def grad_w_tile(i, carry):
        at = pl.ds(pl.multiple_of(i * tile, tile), tile)
        grad_w_o[at, :] = tn(slot_in[:, at], pre_grad[...]).astype(BF16)
        return carry

    lax.fori_loop(0, grad_w_o.shape[0] // tile, grad_w_tile, 0)

    def both_halves(ref):
        total = ref[:n_ep].astype(F32) + ref[n_ep:].astype(F32)
        return [total[:, b, :].astype(BF16) for b in range(images)]

    wait_blocks(out_r, n_all - 1, recv_sem.at[OUT])
    slot_out = both_halves(out_r)
    shares = []
    for b in range(images):
        dot = nt(slot_out[b], grad[b])
        shares.append(combine[b] * (dot - jnp.sum(combine[b] * dot, axis=0, keepdims=True)))
    wait_blocks(in_r, n_all - 1, recv_sem.at[IN])
    slot_in_grad = both_halves(in_r)
    swaps = []
    for b in range(images):
        dot = nt(slot_in_grad[b], tok[b])
        lg_s[b] = shares[b] + dispatch[b] * (
            dot - jnp.sum(dispatch[b] * dot, axis=1, keepdims=True)
        )
        swaps.append(to_partner(lg_s.at[b], lg_r.at[b], SINGLE + images + b))
        swaps[b].start()
    logit_b, share = [], 0.0
    for b in range(images):
        swaps[b].wait()
        logit_b.append((lg_s[b] + lg_r[b]).astype(BF16))
        share += nn(logit_b[b], tok[b])

    rs_s[...] = share.reshape(n_ep, experts // n_ep, width)
    rs_r[ep] = rs_s[ep]
    send_row(lambda to_ep: rs_s.at[to_ep], rs_r, SCATTER)

    def tokens_of(b):
        left = jnp.concatenate([dispatch_b[b], logit_b[b]], axis=0)
        right = jnp.concatenate([slot_in_grad[b], router_t], axis=0)
        grad_tokens_o[b] = tn(left, right).astype(BF16)

    for b in range(images // 2):
        tokens_of(b)
    wait_blocks(rs_r, n_ep - 1, recv_sem.at[SCATTER])
    ag[ep] = jnp.sum(rs_r[...], axis=0)
    send_row(lambda to_ep: ag.at[ep], ag, GATHER)
    for b in range(images // 2, images):
        tokens_of(b)
    wait_blocks(ag, n_ep - 1, recv_sem.at[GATHER])
    grad_router_o[...] = ag[...].reshape(experts, width)

    wait_blocks(slots_r, n_all - 1, send_sem.at[SLOTS])
    wait_blocks(grads_r, n_all - 1, send_sem.at[GRADS])
    wait_blocks(out_r, n_all - 1, send_sem.at[OUT])
    wait_blocks(in_r, n_all - 1, send_sem.at[IN])
    wait_blocks(rs_r, n_ep - 1, send_sem.at[SCATTER])
    wait_blocks(ag, n_ep - 1, send_sem.at[GATHER])


def write_out(tokens_v, router_v, w_v, tokens_o, router_o, w_o, sem):
    cut = w_v.shape[0] // 4
    pairs = [(w_v.at[pl.ds(i * cut, cut)], w_o.at[pl.ds(i * cut, cut)]) for i in range(4)]
    pairs += [(tokens_v, tokens_o), (router_v, router_o)]
    copies = [pltpu.make_async_copy(a, b, sem.at[i]) for i, (a, b) in enumerate(pairs)]
    for copy in copies:
        copy.start()
    for copy in copies:
        copy.wait()


def on_device(n_ep, tokens, router, w_in, w_out, grad_out):
    images, patches, width = tokens.shape
    experts = router.shape[1]
    w_in, w_out = w_in[0], w_out[0]
    model, hidden = w_in.shape
    rows = n_ep * images
    n_all = 2 * n_ep
    vmem = pltpu.VMEM
    grad_tokens, grad_router, grad_w = pl.pallas_call(
        functools.partial(kernel, n_ep),
        out_shape=(
            pltpu.VMEM(tokens.shape, BF16),
            pltpu.VMEM((experts, width), F32),
            pltpu.VMEM(w_in.shape, BF16),
        ),
        in_specs=[pl.BlockSpec(memory_space=pltpu.HBM)] * 5,
        out_specs=(pl.BlockSpec(memory_space=pltpu.VMEM),) * 3,
        scratch_shapes=[
            vmem(tokens.shape, BF16),
            vmem((experts, width), BF16),
            vmem(w_in.shape, BF16),
            vmem(w_out.shape, BF16),
            vmem(grad_out.shape, BF16),
            vmem((images, experts, patches), F32),
            vmem((images, experts, patches), F32),
            vmem((experts, images, width), BF16),
            vmem((n_all, images, width), BF16),
            vmem((experts, images, width), BF16),
            vmem((n_all, images, width), BF16),
            vmem((rows, model), BF16),
            vmem((rows, model), BF16),
            vmem((rows, hidden), BF16),
            vmem((rows, hidden), BF16),
            vmem((rows, hidden), F32),
            vmem((rows, model), F32),
            vmem((n_all, images, width), BF16),
            vmem((n_all, images, width), BF16),
            vmem((n_all, images, width), BF16),
            vmem((n_all, images, width), BF16),
            vmem((images, experts, patches), F32),
            vmem((images, experts, patches), F32),
            vmem((n_ep, experts // n_ep, width), F32),
            vmem((n_ep, experts // n_ep, width), F32),
            vmem((n_ep, experts // n_ep, width), F32),
            pltpu.SemaphoreType.DMA((5,)),
            pltpu.SemaphoreType.DMA((SINGLE + 2 * images,)),
            pltpu.SemaphoreType.DMA((SINGLE + 2 * images,)),
        ],
        compiler_params=pltpu.CompilerParams(
            collective_id=0, has_side_effects=True, vmem_limit_bytes=40 * 1024 * 1024
        ),
    )(*(pltpu.with_memory_space_constraint(x, pltpu.HBM) for x in (tokens, router.T, w_in, w_out, grad_out)))
    results = (grad_tokens, grad_router, grad_w)
    grad_tokens, grad_router, grad_w = pl.pallas_call(
        write_out,
        out_shape=tuple(jax.ShapeDtypeStruct(x.shape, x.dtype) for x in results),
        in_specs=[pl.BlockSpec(memory_space=pltpu.VMEM)] * 3,
        out_specs=(pl.BlockSpec(memory_space=pltpu.HBM),) * 3,
        scratch_shapes=[pltpu.SemaphoreType.DMA((6,))],
        compiler_params=pltpu.CompilerParams(vmem_limit_bytes=8 * 1024 * 1024),
    )(*(pltpu.with_memory_space_constraint(x, pltpu.VMEM) for x in results))
    return grad_tokens, grad_router.T, grad_w.reshape(1, model, hidden)


def solution(mesh):
    placed = (
        P("ep", None, "tp"),
        P("tp", None),
        P("ep", None, "tp"),
        P("ep", "tp", None),
        P("ep", None, "tp"),
    )
    return jax.shard_map(
        functools.partial(on_device, mesh.shape["ep"]),
        mesh=mesh,
        in_specs=placed,
        out_specs=(P("ep", None, "tp"), P("tp", None), P("ep", None, "tp")),
        check_vma=False,
    )
```
